128 devices in a mesh: dp: 32 (over z, x, core), col: 4 (over y).
Axes of the slice: x: 4, y: 4, z: 4, core: 2. Of those that a mesh axis runs over, the one named last changes fastest.
Arguments:
- activations: bfloat16 [16384, 16384], P('dp', 'col'), may hold values from -18 to 18
- out_grads: bfloat16 [16384, 53248], P('dp', 'col'), may hold values from -18 to 18
- sketch: bfloat16 [53248, 128], P('col'), may hold values from -6 to 6
Outputs:
- adapter_b: float32 [16384, 64], P(('col', 'dp'))
- adapter_a_t: float32 [53248, 64], P(('col', 'dp'))
The draws below stay inside these ranges and needn't reach their ends.
All inputs are finite; a program needn't handle non-finite values.
Results may differ from the reference program's by a relative error of at most 0.005.
Values may be sent and summed in bfloat16 or wider, within the bound.
A program may use at most 128 MiB of HBM per device.

```python
import jax
import jax.numpy as jnp
from jax import lax

D = 16384
F = 53248
K = 128
RANK = 64
ITERS = 2
TOK_DEV = 512
TOKENS = 16384


spread_ratio = 30.0


def spiked_field(key, rows, columns, block_rows):
    key_base = jax.random.fold_in(key, 11)
    key_perm = jax.random.fold_in(key, 12)
    values = jax.random.truncated_normal(key_base, -6.0, 6.0, (rows, columns), jnp.float32)
    blocks = rows // block_rows
    pairing = jax.random.permutation(key_perm, blocks)
    row_block = jnp.arange(rows, dtype=jnp.int32) // block_rows
    col_block = jnp.arange(columns, dtype=jnp.int32) // (columns // blocks) % blocks
    chosen = pairing[row_block]
    boost = jnp.where(chosen[:, None] == col_block[None, :], 3.0, 1.0).astype(jnp.float32)
    return values * boost


def drawn_part(key, columns, salt_value):
    key_tokens = jax.random.fold_in(key, 404)
    key_direction = jax.random.fold_in(key, salt_value)
    planted_count = 2 * K
    token_vectors = jax.random.truncated_normal(key_tokens, -3.0, 3.0, (TOKENS, planted_count), jnp.float32)
    directions = jax.random.truncated_normal(key_direction, -3.0, 3.0, (columns, planted_count), jnp.float32)
    position = jnp.arange(planted_count, dtype=jnp.float32)
    amplitude = jnp.exp(-0.5 * jnp.log(jnp.float32(spread_ratio)) * position / K)
    amplitude = amplitude / jnp.sqrt(jnp.sum(amplitude * amplitude))
    return jnp.dot(token_vectors * amplitude[None, :], directions.T, precision=lax.Precision.HIGHEST, preferred_element_type=jnp.float32)


def draw_activations(key, part):
    noisy = spiked_field(jax.random.fold_in(key, 101), TOKENS, D, TOK_DEV)
    total = noisy + drawn_part(key, D, 505)
    return jnp.clip(total, -18.0, 18.0).astype(jnp.bfloat16)


def draw_out_grads(key, part):
    noisy = spiked_field(jax.random.fold_in(key, 202), TOKENS, F, TOK_DEV)
    total = noisy + drawn_part(key, F, 606)
    return jnp.clip(total, -18.0, 18.0).astype(jnp.bfloat16)


def draw_sketch(key, part):
    key_base = jax.random.fold_in(key, 303)
    values = jax.random.truncated_normal(key_base, -6.0, 6.0, (F, K), jnp.float32)
    return values.astype(jnp.bfloat16)


def setup_inputs(seed: int = 0) -> dict:
    arg_keys = jax.random.split(jax.random.key(seed), 4)
    activations = draw_activations(jax.random.fold_in(arg_keys[3], 71), 0)
    out_grads = draw_out_grads(jax.random.fold_in(arg_keys[3], 71), 0)
    sketch = draw_sketch(jax.random.fold_in(arg_keys[3], 71), 0)
    return dict(activations=activations, out_grads=out_grads, sketch=sketch)


def cholesky_basis(panel_in, row_total):
    width = panel_in.shape[1]
    gram_matrix = jnp.dot(panel_in.T.astype(jnp.float32), panel_in.astype(jnp.float32), precision=lax.Precision.HIGHEST, preferred_element_type=jnp.float32)
    identity_k = jnp.eye(width, dtype=jnp.float32)
    shift_value = 1e-05 * jnp.trace(gram_matrix) / width
    lower_factor = jnp.linalg.cholesky(gram_matrix + shift_value * identity_k)
    inverse = jax.scipy.linalg.solve_triangular(lower_factor, identity_k, lower=True)
    scaled = jnp.dot(panel_in.astype(jnp.float32), inverse.T.astype(jnp.float32), precision=lax.Precision.HIGHEST, preferred_element_type=jnp.float32)
    return scaled * jnp.float32(row_total ** 0.5)

def reference(activations, out_grads, sketch):
    right_b = sketch
    left_q = None
    right_p = None
    for iteration in range(ITERS):
        left_s = jnp.dot(out_grads.astype(jnp.float32), right_b.astype(jnp.float32), preferred_element_type=jnp.float32).astype(jnp.bfloat16)
        left_y = lax.dot_general(activations.astype(jnp.float32), left_s.astype(jnp.float32), (((0,), (0,)), ((), ())), preferred_element_type=jnp.float32)
        left_q = cholesky_basis(left_y, D)
        right_t = jnp.dot(activations.astype(jnp.float32), left_q.astype(jnp.bfloat16).astype(jnp.float32), preferred_element_type=jnp.float32).astype(jnp.bfloat16)
        right_z = lax.dot_general(out_grads.astype(jnp.float32), right_t.astype(jnp.float32), (((0,), (0,)), ((), ())), preferred_element_type=jnp.float32)
        right_p = cholesky_basis(right_z, F)
        right_b = right_p.astype(jnp.bfloat16)
    return (left_q[:, :RANK], right_p[:, RANK:])
```

```python
import functools

import jax
import jax.numpy as jnp
from jax import lax
from jax.experimental import pallas as pl
from jax.experimental.pallas import tpu as pltpu
from jax.sharding import PartitionSpec as P

RANK = 64
ITERS = 2
K = 128
f32 = jnp.float32
bf16 = jnp.bfloat16
HIGHEST = lax.Precision.HIGHEST
SIDE = 4


def lanes_of(x, k):
    return jnp.broadcast_to(x[:, k : k + 1], (8, K))


def row_of(x, k):
    return jnp.broadcast_to(x[k : k + 1, :], (8, K))


def inverse_factor(matrix):
    lane = lax.broadcasted_iota(jnp.int32, (8, K), 1)
    sub = lax.broadcasted_iota(jnp.int32, (8, K), 0)
    low = lane < 8
    eye = jnp.where(lane == sub, 1.0, 0.0).astype(f32)

    def block(limit):
        def step(b, rows):
            pivots = [lanes_of(rows[0], k) for k in range(8)]
            panel = jnp.where(low, eye, rows[0])
            recip, coef, done = [], {}, []
            scale = jnp.zeros((8, K), f32)
            for k in range(8):
                d = row_of(pivots[k], k)
                recip.append(1.0 / d)
                scale = jnp.where(sub == k, lax.rsqrt(d), scale)
                done.append(row_of(panel, k))
                if k < 7:
                    c = jnp.where(sub > k, pivots[k] * recip[k], 0.0)
                    for m in range(k + 1, 8):
                        coef[k, m] = row_of(pivots[m], k)
                        pivots[m] = pivots[m] - c * coef[k, m]
                    panel = panel - c * done[k]
            new = [panel * scale]
            for u in range(1, 16):
                if u >= limit:
                    new.append(rows[u])
                    continue
                cols = [lanes_of(rows[u], k) for k in range(8)]
                acc = jnp.where(low, 0.0, rows[u])
                for k in range(8):
                    ck = cols[k] * recip[k]
                    for m in range(k + 1, 8):
                        cols[m] = cols[m] - ck * coef[k, m]
                    acc = acc - ck * done[k]
                new.append(jnp.where(u < 16 - b, acc, rows[u]))
            new = [pltpu.roll(w, K - 8, 1) for w in new]
            return tuple(new[1:] + new[:1])

        return step

    rows = tuple(matrix[8 * u : 8 * u + 8, :] for u in range(16))
    for part in range(4):
        rows = lax.fori_loop(4 * part, 4 * part + 4, block(16 - 4 * part), rows)
    whole = jnp.concatenate(rows, axis=0)
    i = lax.broadcasted_iota(jnp.int32, (K, K), 0)
    j = lax.broadcasted_iota(jnp.int32, (K, K), 1)
    return jnp.where(j <= i, whole, 0.0)


def kernel(
    features, hidden, a_hbm, o_hbm, sk_hbm, q_ref, p_ref,
    a, o, sketch, load_sem,
    s_part, s_recv, s_mine, s_all, s_t, s_sem,
    gram_own, gram_first, gram_slots, gram_half, gram_all, gram_sem, factor_y, factor_z,
    *panel_refs,
):
    dp, y = lax.axis_index("dp"), lax.axis_index("col")
    z, x, c = dp // 8, lax.rem(dp // 2, SIDE), lax.rem(dp, 2)
    names = ("own", "c1s", "c1r", "a2s", "a2r", "b2s", "b2r", "a3s", "a3r", "b3s", "b3r", "shard", "gathered", "sem")
    half = len(names)
    bufs_y = dict(zip(names, panel_refs[:half]))
    bufs_z = dict(zip(names, panel_refs[half:]))

    def at(z_=None, x_=None, c_=None):
        z_ = z if z_ is None else z_
        x_ = x if x_ is None else x_
        c_ = c if c_ is None else c_
        return {"dp": (z_ * SIDE + x_) * 2 + c_, "col": y}

    def along(axis, j):
        if axis == "x":
            return at(x_=lax.rem(x + j, SIDE))
        if axis == "z":
            return at(z_=lax.rem(z + j, SIDE))
        if axis == "y":
            return {"dp": dp, "col": lax.rem(y + j, SIDE)}
        return at(c_=1 - c)

    pending = []

    def send(src, dst, sems, index, device):
        copy = pltpu.make_async_remote_copy(
            src_ref=src, dst_ref=dst, send_sem=sems.at[0, index], recv_sem=sems.at[1, index],
            device_id=device, device_id_type=pl.DeviceIdType.MESH,
        )
        copy.start()
        pending.append(copy)
        return copy

    def flush():
        for copy in pending:
            copy.wait_send()
        pending.clear()

    tokens = s_mine.shape[0]
    turn = [lax.rem(y + 1 + k, SIDE) for k in range(SIDE)]
    loads = [pltpu.make_async_copy(sk_hbm, sketch, load_sem.at[0])]
    for k in range(SIDE):
        span = pl.ds(pl.multiple_of(turn[k] * tokens, tokens), tokens)
        loads.append(pltpu.make_async_copy(o_hbm.at[span, :], o.at[span, :], load_sem.at[1 + k]))
    loads.append(pltpu.make_async_copy(a_hbm, a, load_sem.at[5]))
    for copy in loads:
        copy.start()

    barrier = pltpu.get_barrier_semaphore()
    partners = [along("core", 0)] + [along(axis, j) for axis in "xyz" for j in (1, 2, 3)]
    for device in partners:
        pl.semaphore_signal(barrier, inc=1, device_id=device, device_id_type=pl.DeviceIdType.MESH)
    pl.semaphore_wait(barrier, len(partners))

    def send_tokens(k):
        span = pl.ds(pl.multiple_of(turn[k] * tokens, tokens), tokens)
        return send(s_part.at[span, :], s_recv.at[k], s_sem, k, along("y", k + 1))

    def share_tokens(sends, factor):
        span = pl.ds(pl.multiple_of(y * tokens, tokens), tokens)
        total = s_part[span, :]
        for k in range(3):
            sends[k].wait_recv()
            total = total + s_recv[k]
        if factor is not None:
            total = lax.dot_general(
                total, factor(), (((1,), (1,)), ((), ())), precision=HIGHEST, preferred_element_type=f32
            )
        s_all[span, :] = total.astype(bf16)
        outs = [send(s_all.at[span, :], s_all.at[span, :], s_sem, 3 + k, along("y", k + 1)) for k in range(3)]
        for copy in outs:
            copy.wait_recv()
        flush()
        s_t[...] = s_all[...].T

    def reduce_panel(weights, bufs, columns):
        own, c1s, c1r, sem = bufs["own"], bufs["c1s"], bufs["c1r"], bufs["sem"]
        rows = own.shape[2]
        h = rows // 2
        zs = [lax.rem(z + 1 + k, SIDE) for k in range(SIDE)]
        span = columns // SIDE
        pieces = 1 if span % 1024 == 0 else 2
        first, second_a, second_b = [], [], []

        def compute(k):
            for piece in range(pieces):
                width = span // pieces
                n = SIDE // pieces
                start = pl.multiple_of(zs[k] * span + piece * width, K)
                r = jnp.dot(s_t[...], weights[:, pl.ds(start, width)], preferred_element_type=f32).T
                r = r.reshape(n, 2, rows, K)
                own[k, piece * n : (piece + 1) * n] = jnp.where(c == 0, r[:, 0], r[:, 1])
                c1s[k, piece * n : (piece + 1) * n] = jnp.where(c == 0, r[:, 1], r[:, 0]).astype(bf16)
            first.append(send(c1s.at[k], c1r.at[k], sem, k, along("core", 0)))

        def pass_on(k):
            first[k].wait_recv()
            for i in range(SIDE):
                v = own[k, i] + c1r[k, i].astype(f32)
                own[k, i] = v
                v = v.astype(bf16)
                bufs["a2s"][k, i] = v[:h]
                bufs["b2s"][k, i] = v[h:]
            for j in (1, 2, 3):
                there = lax.rem(x + j, SIDE)
                second_a.append(
                    send(bufs["a2s"].at[k, there], bufs["a2r"].at[k, j - 1], sem, 4 + k * 3 + j - 1, along("x", j))
                )
            if k < 3:
                second_b.append(send(bufs["b2s"].at[k], bufs["b2r"].at[k], sem, 16 + k, along("z", k + 1)))

        for k in range(SIDE):
            compute(k)
            if k > 0:
                pass_on(k - 1)
        pass_on(3)
        third_a, third_b = [], []
        for k in range(SIDE):
            total = own[k, x, :h, :]
            for j in range(3):
                second_a[k * 3 + j].wait_recv()
                total = total + bufs["a2r"][k, j].astype(f32)
            if k < 3:
                bufs["a3s"][k] = total.astype(bf16)
                third_a.append(send(bufs["a3s"].at[k], bufs["a3r"].at[k], sem, 19 + k, along("z", k + 1)))
            else:
                mine_a = total
        for k in range(3):
            second_b[k].wait_recv()
        for k in range(SIDE):
            there = lax.rem(x + 1 + k, SIDE)
            total = own[3, there, h:, :]
            for j in range(3):
                total = total + bufs["b2r"][j, there].astype(f32)
            if k < 3:
                bufs["b3s"][k] = total.astype(bf16)
                third_b.append(send(bufs["b3s"].at[k], bufs["b3r"].at[k], sem, 22 + k, along("x", k + 1)))
            else:
                mine_b = total
        for k in range(3):
            third_a[k].wait_recv()
            mine_a = mine_a + bufs["a3r"][k].astype(f32)
        bufs["shard"][:h, :] = mine_a
        for k in range(3):
            third_b[k].wait_recv()
            mine_b = mine_b + bufs["b3r"][k].astype(f32)
        bufs["shard"][h:, :] = mine_b
        flush()

    def gram_steps(bufs):
        part = bufs["shard"][...]
        gram_own[...] = lax.dot_general(
            part, part, (((0,), (0,)), ((), ())), precision=HIGHEST, preferred_element_type=f32
        )
        h = K // 2
        mine = pl.ds(pl.multiple_of(c * h, h), h)
        theirs = pl.ds(pl.multiple_of((1 - c) * h, h), h)
        copy = send(gram_own.at[theirs, :], gram_first, gram_sem, 0, along("core", 0))
        yield
        copy.wait_recv()
        total = gram_own[mine, :] + gram_first[...]
        for stage, (axis, place) in enumerate((("x", x), ("z", z), ("y", y))):
            gram_slots[stage, place] = total
            copies = [
                send(gram_slots.at[stage, place], gram_slots.at[stage, place], gram_sem, 1 + 3 * stage + j - 1, along(axis, j))
                for j in (1, 2, 3)
            ]
            yield
            for copy in copies:
                copy.wait_recv()
            total = gram_slots[stage, 0] + gram_slots[stage, 1] + gram_slots[stage, 2] + gram_slots[stage, 3]
        gram_half[...] = total
        gram_all[mine, :] = total
        copy = send(gram_half, gram_all.at[mine, :], gram_sem, 10, along("core", 0))
        yield
        copy.wait_recv()
        yield

    def factor_from_gram(row_total, out):
        g = gram_all[...]
        i = lax.broadcasted_iota(jnp.int32, (K, K), 0)
        j = lax.broadcasted_iota(jnp.int32, (K, K), 1)
        on_diagonal = jnp.where(i == j, g, 0.0)
        shift = 1e-5 * jnp.sum(jnp.sum(on_diagonal, axis=1, keepdims=True), axis=0, keepdims=True) / K
        out[...] = inverse_factor(g + jnp.where(i == j, shift, 0.0)) * f32(row_total**0.5)

    def gather_panel(bufs, steps):
        g, sem, shard = bufs["gathered"], bufs["sem"], bufs["shard"]
        h = shard.shape[0] // 2
        g[z, x, c] = shard[...].astype(bf16)
        top, bottom = pl.ds(0, h), pl.ds(h, h)

        def piece(z_, x_, part):
            return g.at[z_, x_, c, part, :]

        base = 25
        a1 = [send(piece(z, x, top), piece(z, x, top), sem, base + j - 1, along("z", j)) for j in (1, 2, 3)]
        b1 = [send(piece(z, x, bottom), piece(z, x, bottom), sem, base + 3 + j - 1, along("x", j)) for j in (1, 2, 3)]
        a2, b2 = {}, {}

        def forward(k):
            from_z, from_x = lax.rem(z - k + SIDE, SIDE), lax.rem(x - k + SIDE, SIDE)
            for j in (1, 2, 3):
                a2[k, j] = send(
                    piece(from_z, x, top), piece(from_z, x, top), sem, base + 6 + k * 3 + j - 1, along("x", j)
                )
                b2[k, j] = send(
                    piece(z, from_x, bottom), piece(z, from_x, bottom), sem, base + 18 + k * 3 + j - 1, along("z", j)
                )

        forward(0)
        next(steps)
        for k in (1, 2, 3):
            a1[k - 1].wait_recv()
            b1[k - 1].wait_recv()
            forward(k)
        cores = []

        def over(ref):
            cores.append(send(ref, ref, sem, base + 30 + len(cores), along("core", 0)))

        over(g.at[:, x, c, top, :])
        over(g.at[z, :, c, bottom, :])
        next(steps)
        for j in (1, 2, 3):
            for k in range(SIDE):
                a2[k, j].wait_recv()
            over(g.at[:, lax.rem(x - j + SIDE, SIDE), c, top, :])
            for k in range(SIDE):
                b2[k, j].wait_recv()
            over(g.at[lax.rem(z - j + SIDE, SIDE), :, c, bottom, :])
            if j < 3:
                next(steps)
        for copy in cores:
            copy.wait_recv()

    row_y, row_z = float(SIDE * features), float(SIDE * hidden)
    for iteration in range(ITERS):
        sends = []
        if iteration == 0:
            loads[0].wait()
            for k in range(SIDE):
                span = pl.ds(pl.multiple_of(turn[k] * tokens, tokens), tokens)
                loads[1 + k].wait()
                s_part[span, :] = jnp.zeros((tokens, K), f32)

                @pl.loop(0, SIDE)
                def _(i):
                    deep = pl.ds(pl.multiple_of(i * (hidden // SIDE), K), hidden // SIDE)
                    s_part[span, :] += jnp.dot(o[span, deep], sketch[deep, :], preferred_element_type=f32)

                if k < 3:
                    sends.append(send_tokens(k))
            loads[5].wait()
            share_tokens(sends, None)
        else:
            s_part[...] = jnp.zeros(s_part.shape, f32)
            n = hidden // SIDE

            @pl.loop(0, SIDE)
            def _(i):
                deep = pl.ds(pl.multiple_of(i * n, K), n)
                block = bufs_z["gathered"][i].reshape(n, K)
                s_part[...] += jnp.dot(o[:, deep], block, preferred_element_type=f32)

            sends = [send_tokens(k) for k in range(3)]
            for _ in steps:
                pass
            factor_from_gram(row_z, factor_z)
            share_tokens(sends, lambda: factor_z[...])
        reduce_panel(a, bufs_y, features)
        steps = gram_steps(bufs_y)
        gather_panel(bufs_y, steps)
        s_part[...] = jnp.dot(a[...], bufs_y["gathered"][...].reshape(features, K), preferred_element_type=f32)
        sends = [send_tokens(k) for k in range(3)]
        for _ in steps:
            pass
        factor_from_gram(row_y, factor_y)
        share_tokens(sends, lambda: factor_y[...])
        if iteration == ITERS - 1:
            q = lax.dot_general(
                bufs_y["shard"][...], factor_y[...], (((1,), (1,)), ((), ())), precision=HIGHEST, preferred_element_type=f32
            )
            q_ref[...] = q[:, :RANK]
        reduce_panel(o, bufs_z, hidden)
        steps = gram_steps(bufs_z)
        if iteration < ITERS - 1:
            gather_panel(bufs_z, steps)
    for _ in steps:
        pass
    factor_from_gram(row_z, factor_z)
    p = lax.dot_general(
        bufs_z["shard"][...], factor_z[...], (((1,), (1,)), ((), ())), precision=HIGHEST, preferred_element_type=f32
    )
    p_ref[...] = p[:, RANK:]
    flush()


def panel_scratch(rows):
    h = rows // 2
    return [
        pltpu.VMEM((4, 4, rows, K), f32),
        pltpu.VMEM((4, 4, rows, K), bf16),
        pltpu.VMEM((4, 4, rows, K), bf16),
        pltpu.VMEM((4, 4, h, K), bf16),
        pltpu.VMEM((4, 3, h, K), bf16),
        pltpu.VMEM((4, 4, h, K), bf16),
        pltpu.VMEM((3, 4, h, K), bf16),
        pltpu.VMEM((3, h, K), bf16),
        pltpu.VMEM((3, h, K), bf16),
        pltpu.VMEM((3, h, K), bf16),
        pltpu.VMEM((3, h, K), bf16),
        pltpu.VMEM((rows, K), f32),
        pltpu.VMEM((4, 4, 2, rows, K), bf16),
        pltpu.SemaphoreType.DMA((2, 64)),
    ]


def body(activations, out_grads, sketch):
    tokens, features = activations.shape
    hidden = out_grads.shape[1]
    devices = lax.axis_size("dp")
    rows_y, rows_z = features // devices, hidden // devices
    quarter = tokens // SIDE
    scratch = [
        pltpu.VMEM((tokens, features), bf16),
        pltpu.VMEM((tokens, hidden), bf16),
        pltpu.VMEM((hidden, K), bf16),
        pltpu.SemaphoreType.DMA((6,)),
        pltpu.VMEM((tokens, K), f32),
        pltpu.VMEM((3, quarter, K), f32),
        pltpu.VMEM((quarter, K), bf16),
        pltpu.VMEM((tokens, K), bf16),
        pltpu.VMEM((K, tokens), bf16),
        pltpu.SemaphoreType.DMA((2, 6)),
        pltpu.VMEM((K, K), f32),
        pltpu.VMEM((K // 2, K), f32),
        pltpu.VMEM((3, SIDE, K // 2, K), f32),
        pltpu.VMEM((K // 2, K), f32),
        pltpu.VMEM((K, K), f32),
        pltpu.SemaphoreType.DMA((2, 11)),
        pltpu.VMEM((K, K), f32),
        pltpu.VMEM((K, K), f32),
        *panel_scratch(rows_y),
        *panel_scratch(rows_z),
    ]
    return pl.pallas_call(
        functools.partial(kernel, features, hidden),
        out_shape=(
            jax.ShapeDtypeStruct((rows_y, RANK), f32),
            jax.ShapeDtypeStruct((rows_z, K - RANK), f32),
        ),
        in_specs=[pl.BlockSpec(memory_space=pl.ANY)] * 3,
        out_specs=(pl.BlockSpec(memory_space=pltpu.VMEM), pl.BlockSpec(memory_space=pltpu.VMEM)),
        scratch_shapes=scratch,
        compiler_params=pltpu.CompilerParams(
            collective_id=0, has_side_effects=True, vmem_limit_bytes=58 << 20
        ),
        name="subspace_iteration",
    )(activations, out_grads, sketch)


def solution(mesh):
    return jax.shard_map(
        body,
        mesh=mesh,
        in_specs=(P("dp", "col"), P("dp", "col"), P("col", None)),
        out_specs=(P(("col", "dp"), None), P(("col", "dp"), None)),
        check_vma=False,
    )
```

```python
import functools

import jax
import jax.numpy as jnp
from jax import lax
from jax.experimental import pallas as pl
from jax.experimental.pallas import tpu as pltpu
from jax.sharding import PartitionSpec as P

RANK = 64
ITERS = 2
K = 128
f32 = jnp.float32
bf16 = jnp.bfloat16
HIGHEST = lax.Precision.HIGHEST
SIDE = 4


def lanes_of(x, k):
    return jnp.broadcast_to(x[:, k : k + 1], (8, K))


def row_of(x, k):
    return jnp.broadcast_to(x[k : k + 1, :], (8, K))


def inverse_factor(matrix):
    lane = lax.broadcasted_iota(jnp.int32, (8, K), 1)
    sub = lax.broadcasted_iota(jnp.int32, (8, K), 0)
    rows = [matrix[8 * u : 8 * u + 8, :] for u in range(16)]
    for b in range(16):
        first = 8 * b
        inside = (lane >= first) & (lane < first + 8)
        pivots = [lanes_of(rows[b], first + k) for k in range(8)]
        panel = jnp.where(inside, jnp.where(lane == sub + first, 1.0, 0.0), rows[b])
        recip, coef, done = [], {}, []
        scale = jnp.zeros((8, K), f32)
        for k in range(8):
            d = row_of(pivots[k], k)
            recip.append(1.0 / d)
            scale = jnp.where(sub == k, lax.rsqrt(d), scale)
            done.append(row_of(panel, k))
            if k < 7:
                c = jnp.where(sub > k, pivots[k] * recip[k], 0.0)
                for m in range(k + 1, 8):
                    coef[k, m] = row_of(pivots[m], k)
                    pivots[m] = pivots[m] - c * coef[k, m]
                panel = panel - c * done[k]
        rows[b] = panel * scale
        for u in range(b + 1, 16):
            cols = [lanes_of(rows[u], first + k) for k in range(8)]
            acc = jnp.where(inside, 0.0, rows[u])
            for k in range(8):
                ck = cols[k] * recip[k]
                for m in range(k + 1, 8):
                    cols[m] = cols[m] - ck * coef[k, m]
                acc = acc - ck * done[k]
            rows[u] = acc
    whole = jnp.concatenate(rows, axis=0)
    i = lax.broadcasted_iota(jnp.int32, (K, K), 0)
    j = lax.broadcasted_iota(jnp.int32, (K, K), 1)
    return jnp.where(j <= i, whole, 0.0)


def wave_rows(rows):
    tiles = rows // 16
    counts = [tiles // 4 + (1 if tiles % 4 > i else 0) for i in (0, 2, 3, 1)]
    spans, first = [], 0
    for count in counts:
        spans.append((first, count * 16))
        first += count * 16
    return (spans[0], spans[1]), (spans[2], spans[3])


def kernel(
    features, hidden, a_hbm, o_hbm, sk_hbm, q_ref, p_ref,
    a, o, sketch, load_sem,
    s_part, s_recv, s_mine, s_all, s_t, s_sem,
    gram_own, gram_first, gram_slots, gram_half, gram_all, gram_sem, factor_y, factor_z,
    *panel_refs,
):
    dp, y = lax.axis_index("dp"), lax.axis_index("col")
    z, x, c = dp // 8, lax.rem(dp // 2, SIDE), lax.rem(dp, 2)
    names = ("own", "c1s", "c1r", "s2", "a2r", "b2r", "s3", "r3", "shard", "gathered", "sem")
    half = len(names)
    bufs_y = dict(zip(names, panel_refs[:half]))
    bufs_z = dict(zip(names, panel_refs[half:]))

    def at(z_=None, x_=None, c_=None):
        z_ = z if z_ is None else z_
        x_ = x if x_ is None else x_
        c_ = c if c_ is None else c_
        return {"dp": (z_ * SIDE + x_) * 2 + c_, "col": y}

    def along(axis, j):
        if axis == "x":
            return at(x_=lax.rem(x + j, SIDE))
        if axis == "z":
            return at(z_=lax.rem(z + j, SIDE))
        if axis == "y":
            return {"dp": dp, "col": lax.rem(y + j, SIDE)}
        return at(c_=1 - c)

    pending = []

    def send(src, dst, sems, index, device):
        copy = pltpu.make_async_remote_copy(
            src_ref=src, dst_ref=dst, send_sem=sems.at[0, index], recv_sem=sems.at[1, index],
            device_id=device, device_id_type=pl.DeviceIdType.MESH,
        )
        copy.start()
        pending.append(copy)
        return copy

    def flush():
        for copy in pending:
            copy.wait_send()
        pending.clear()

    barrier = pltpu.get_barrier_semaphore()
    partners = [along("core", 0)] + [along(axis, j) for axis in "xyz" for j in (1, 2, 3)]
    for device in partners:
        pl.semaphore_signal(barrier, inc=1, device_id=device, device_id_type=pl.DeviceIdType.MESH)

    tokens = s_mine.shape[0]
    turn = [lax.rem(y + 1 + k, SIDE) for k in range(SIDE)]
    loads = [pltpu.make_async_copy(sk_hbm, sketch, load_sem.at[0])]
    for k in range(SIDE):
        span = pl.ds(pl.multiple_of(turn[k] * tokens, tokens), tokens)
        loads.append(pltpu.make_async_copy(o_hbm.at[span, :], o.at[span, :], load_sem.at[1 + k]))
    loads.append(pltpu.make_async_copy(a_hbm, a, load_sem.at[5]))
    for copy in loads:
        copy.start()

    def send_tokens(k):
        span = pl.ds(pl.multiple_of(turn[k] * tokens, tokens), tokens)
        return send(s_part.at[span, :], s_recv.at[k], s_sem, k, along("y", k + 1))

    def share_tokens(sends, factor):
        span = pl.ds(pl.multiple_of(y * tokens, tokens), tokens)
        total = s_part[span, :]
        for k in range(3):
            sends[k].wait_recv()
            total = total + s_recv[k]
        if factor is not None:
            total = lax.dot_general(
                total, factor(), (((1,), (1,)), ((), ())), precision=HIGHEST, preferred_element_type=f32
            )
        s_all[span, :] = total.astype(bf16)
        outs = [send(s_all.at[span, :], s_all.at[span, :], s_sem, 3 + k, along("y", k + 1)) for k in range(3)]
        for copy in outs:
            copy.wait_recv()
        flush()
        s_t[...] = s_all[...].T

    def gram_steps(bufs):
        part = bufs["shard"][...]
        gram_own[...] = lax.dot_general(
            part, part, (((0,), (0,)), ((), ())), precision=HIGHEST, preferred_element_type=f32
        )
        h = K // 2
        mine = pl.ds(pl.multiple_of(c * h, h), h)
        theirs = pl.ds(pl.multiple_of((1 - c) * h, h), h)
        copy = send(gram_own.at[theirs, :], gram_first, gram_sem, 0, along("core", 0))
        yield
        copy.wait_recv()
        total = gram_own[mine, :] + gram_first[...]
        thirds = ((0, 24, "xzy"), (24, 24, "zyx"), (48, 16, "yxz"))
        places = {"x": x, "z": z, "y": y}
        totals = [total[first : first + count] for first, count, _ in thirds]
        for stage in range(3):
            copies = []
            for part, (first, count, order) in enumerate(thirds):
                span, place = pl.ds(first, count), places[order[stage]]
                gram_slots[stage, place, span, :] = totals[part]
                for j in (1, 2, 3):
                    ref = gram_slots.at[stage, place, span, :]
                    copies.append(send(ref, ref, gram_sem, 2 + 9 * stage + 3 * part + j - 1, along(order[stage], j)))
            yield
            for part, (first, count, order) in enumerate(thirds):
                for copy in copies[3 * part : 3 * part + 3]:
                    copy.wait_recv()
                terms = [gram_slots[stage, i, first : first + count, :] for i in range(SIDE)]
                totals[part] = terms[0] + terms[1] + terms[2] + terms[3]
        total = jnp.concatenate(totals, axis=0)
        gram_half[...] = total
        gram_all[mine, :] = total
        copy = send(gram_half, gram_all.at[mine, :], gram_sem, 1, along("core", 0))
        yield
        copy.wait_recv()
        yield

    def factor_from_gram(row_total, out):
        g = gram_all[...]
        i = lax.broadcasted_iota(jnp.int32, (K, K), 0)
        j = lax.broadcasted_iota(jnp.int32, (K, K), 1)
        on_diagonal = jnp.where(i == j, g, 0.0)
        shift = 1e-5 * jnp.sum(jnp.sum(on_diagonal, axis=1, keepdims=True), axis=0, keepdims=True) / K
        out[...] = inverse_factor(g + jnp.where(i == j, shift, 0.0)) * f32(row_total**0.5)

    def pass_panel(weights, bufs, columns, gather):
        own, c1s, c1r, s2, sem = bufs["own"], bufs["c1s"], bufs["c1r"], bufs["s2"], bufs["sem"]
        a2r, b2r, s3, r3, shard, g = bufs["a2r"], bufs["b2r"], bufs["s3"], bufs["r3"], bufs["shard"], bufs["gathered"]
        rows = own.shape[2]
        waves = wave_rows(rows)
        zs = [lax.rem(z + 1 + k, SIDE) for k in range(SIDE)]
        span = columns // SIDE
        pieces = 1 if span % 1024 == 0 else 2
        first = []

        def compute(k):
            for piece in range(pieces):
                width = span // pieces
                n = SIDE // pieces
                start = pl.multiple_of(zs[k] * span + piece * width, K)
                r = jnp.dot(s_t[...], weights[:, pl.ds(start, width)], preferred_element_type=f32).T
                r = r.reshape(n, 2, rows, K)
                own[k, piece * n : (piece + 1) * n] = jnp.where(c == 0, r[:, 0], r[:, 1])
                c1s[k, piece * n : (piece + 1) * n] = jnp.where(c == 0, r[:, 1], r[:, 0]).astype(bf16)
            first.append(send(c1s.at[k], c1r.at[k], sem, k, along("core", 0)))

        def add_core(k):
            first[k].wait_recv()
            for i in range(SIDE):
                v = own[k, i] + c1r[k, i].astype(f32)
                own[k, i] = v
                s2[k, i] = v.astype(bf16)

        class Wave:
            def __init__(self, index):
                self.a, self.b = waves[index]
                self.base = 4 + 59 * index
                self.second_a, self.second_b, self.third_a, self.third_b = [], [], [], []
                self.gather_a, self.gather_b, self.on_a, self.on_b, self.cores = [], [], {}, {}, []

            def second(self, k):
                for j in (1, 2, 3):
                    there = lax.rem(x + j, SIDE)
                    self.second_a.append(
                        send(
                            s2.at[k, there, pl.ds(*self.a), :], a2r.at[k, j - 1, pl.ds(*self.a), :],
                            sem, self.base + k * 3 + j - 1, along("x", j),
                        )
                    )
                if k < 3:
                    self.second_b.append(
                        send(
                            s2.at[k, :, pl.ds(*self.b), :], b2r.at[k, :, pl.ds(*self.b), :],
                            sem, self.base + 12 + k, along("z", k + 1),
                        )
                    )

            def third(self):
                part = pl.ds(*self.a)
                for k in range(SIDE):
                    total = own[k, x, part, :]
                    for j in range(3):
                        self.second_a[k * 3 + j].wait_recv()
                        total = total + a2r[k, j, part, :].astype(f32)
                    if k < 3:
                        s3[k, part, :] = total.astype(bf16)
                        self.third_a.append(
                            send(s3.at[k, part, :], r3.at[k, part, :], sem, self.base + 15 + k, along("z", k + 1))
                        )
                    else:
                        shard[part, :] = total
                part = pl.ds(*self.b)
                for k in range(3):
                    self.second_b[k].wait_recv()
                for k in range(SIDE):
                    there = lax.rem(x + 1 + k, SIDE)
                    total = own[3, there, part, :]
                    for j in range(3):
                        total = total + b2r[j, there, part, :].astype(f32)
                    if k < 3:
                        s3[k, part, :] = total.astype(bf16)
                        self.third_b.append(
                            send(s3.at[k, part, :], r3.at[k, part, :], sem, self.base + 18 + k, along("x", k + 1))
                        )
                    else:
                        shard[part, :] = total

            def piece(self, z_, x_, part):
                return g.at[z_, x_, c, pl.ds(*part), :]

            def finish(self):
                for part, copies in ((self.a, self.third_a), (self.b, self.third_b)):
                    part = pl.ds(*part)
                    total = shard[part, :]
                    for k in range(3):
                        copies[k].wait_recv()
                        total = total + r3[k, part, :].astype(f32)
                    shard[part, :] = total
                    if gather:
                        g[z, x, c, part, :] = total.astype(bf16)
                        axis, part, base, outs = (
                            ("z", self.a, 21, self.gather_a) if copies is self.third_a else ("x", self.b, 24, self.gather_b)
                        )
                        for j in (1, 2, 3):
                            ref = self.piece(z, x, part)
                            outs.append(send(ref, ref, sem, self.base + base + j - 1, along(axis, j)))
                if gather:
                    self.forward(0)

            def forward(self, k):
                if k > 0:
                    self.gather_a[k - 1].wait_recv()
                    self.gather_b[k - 1].wait_recv()
                from_z, from_x = lax.rem(z - k + SIDE, SIDE), lax.rem(x - k + SIDE, SIDE)
                for j in (1, 2, 3):
                    ref = self.piece(from_z, x, self.a)
                    self.on_a[k, j] = send(ref, ref, sem, self.base + 27 + k * 3 + j - 1, along("x", j))
                    ref = self.piece(z, from_x, self.b)
                    self.on_b[k, j] = send(ref, ref, sem, self.base + 39 + k * 3 + j - 1, along("z", j))

            def over(self, ref):
                self.cores.append(send(ref, ref, sem, self.base + 51 + len(self.cores), along("core", 0)))

            def first_hop(self):
                for k in (1, 2, 3):
                    self.forward(k)
                self.over(g.at[:, x, c, pl.ds(*self.a), :])
                self.over(g.at[z, :, c, pl.ds(*self.b), :])

            def second_hop(self):
                for j in (1, 2, 3):
                    for k in range(SIDE):
                        self.on_a[k, j].wait_recv()
                    self.over(g.at[:, lax.rem(x - j + SIDE, SIDE), c, pl.ds(*self.a), :])
                    for k in range(SIDE):
                        self.on_b[k, j].wait_recv()
                    self.over(g.at[lax.rem(z - j + SIDE, SIDE), :, c, pl.ds(*self.b), :])

            def wait_cores(self):
                for copy in self.cores:
                    copy.wait_recv()

        one, two = Wave(0), Wave(1)
        for k in range(SIDE):
            compute(k)
            if k > 0:
                add_core(k - 1)
                one.second(k - 1)
        add_core(3)
        one.second(3)
        for k in range(SIDE):
            two.second(k)
        one.third()
        if rows > 256:
            one.finish()
            two.third()
        else:
            two.third()
            one.finish()
        if gather and rows > 256:
            one.first_hop()
        two.finish()
        steps = gram_steps(bufs)
        if not gather:
            return steps
        next(steps)
        next(steps)
        if rows <= 256:
            one.first_hop()
        two.first_hop()
        next(steps)
        one.second_hop()
        two.second_hop()
        next(steps)
        one.wait_cores()
        two.wait_cores()
        return steps

    row_y, row_z = float(SIDE * features), float(SIDE * hidden)
    for iteration in range(ITERS):
        sends = []
        if iteration == 0:
            loads[0].wait()
            for k in range(SIDE):
                span = pl.ds(pl.multiple_of(turn[k] * tokens, tokens), tokens)
                loads[1 + k].wait()
                s_part[span, :] = jnp.zeros((tokens, K), f32)

                @pl.loop(0, SIDE)
                def _(i):
                    deep = pl.ds(pl.multiple_of(i * (hidden // SIDE), K), hidden // SIDE)
                    s_part[span, :] += jnp.dot(o[span, deep], sketch[deep, :], preferred_element_type=f32)

                if k == 0:
                    pl.semaphore_wait(barrier, len(partners))
                if k < 3:
                    sends.append(send_tokens(k))
            loads[5].wait()
            share_tokens(sends, None)
        else:
            s_part[...] = jnp.zeros(s_part.shape, f32)
            n = hidden // SIDE

            @pl.loop(0, SIDE)
            def _(i):
                deep = pl.ds(pl.multiple_of(i * n, K), n)
                block = bufs_z["gathered"][i].reshape(n, K)
                s_part[...] += jnp.dot(o[:, deep], block, preferred_element_type=f32)

            sends = [send_tokens(k) for k in range(3)]
            for _ in steps:
                pass
            factor_from_gram(row_z, factor_z)
            share_tokens(sends, lambda: factor_z[...])
        steps = pass_panel(a, bufs_y, features, True)
        s_part[...] = jnp.dot(a[...], bufs_y["gathered"][...].reshape(features, K), preferred_element_type=f32)
        sends = [send_tokens(k) for k in range(3)]
        for _ in steps:
            pass
        factor_from_gram(row_y, factor_y)
        share_tokens(sends, lambda: factor_y[...])
        if iteration == ITERS - 1:
            q = lax.dot_general(
                factor_y[...], bufs_y["shard"][...], (((1,), (1,)), ((), ())), precision=HIGHEST, preferred_element_type=f32
            )
            q_ref[...] = q[:RANK, :]
        steps = pass_panel(o, bufs_z, hidden, iteration < ITERS - 1)
    for _ in steps:
        pass
    factor_from_gram(row_z, factor_z)
    p = lax.dot_general(
        factor_z[...], bufs_z["shard"][...], (((1,), (1,)), ((), ())), precision=HIGHEST, preferred_element_type=f32
    )
    p_ref[...] = p[RANK:, :]
    flush()


def panel_scratch(rows):
    return [
        pltpu.VMEM((4, 4, rows, K), f32),
        pltpu.VMEM((4, 4, rows, K), bf16),
        pltpu.VMEM((4, 4, rows, K), bf16),
        pltpu.VMEM((4, 4, rows, K), bf16),
        pltpu.VMEM((4, 3, rows, K), bf16),
        pltpu.VMEM((3, 4, rows, K), bf16),
        pltpu.VMEM((3, rows, K), bf16),
        pltpu.VMEM((3, rows, K), bf16),
        pltpu.VMEM((rows, K), f32),
        pltpu.VMEM((4, 4, 2, rows, K), bf16),
        pltpu.SemaphoreType.DMA((2, 122)),
    ]


def body(activations, out_grads, sketch):
    tokens, features = activations.shape
    hidden = out_grads.shape[1]
    devices = lax.axis_size("dp")
    rows_y, rows_z = features // devices, hidden // devices
    quarter = tokens // SIDE
    scratch = [
        pltpu.VMEM((tokens, features), bf16),
        pltpu.VMEM((tokens, hidden), bf16),
        pltpu.VMEM((hidden, K), bf16),
        pltpu.SemaphoreType.DMA((6,)),
        pltpu.VMEM((tokens, K), f32),
        pltpu.VMEM((3, quarter, K), f32),
        pltpu.VMEM((quarter, K), bf16),
        pltpu.VMEM((tokens, K), bf16),
        pltpu.VMEM((K, tokens), bf16),
        pltpu.SemaphoreType.DMA((2, 6)),
        pltpu.VMEM((K, K), f32),
        pltpu.VMEM((K // 2, K), f32),
        pltpu.VMEM((3, SIDE, K // 2, K), f32),
        pltpu.VMEM((K // 2, K), f32),
        pltpu.VMEM((K, K), f32),
        pltpu.SemaphoreType.DMA((2, 29)),
        pltpu.VMEM((K, K), f32),
        pltpu.VMEM((K, K), f32),
        *panel_scratch(rows_y),
        *panel_scratch(rows_z),
    ]
    q, p = pl.pallas_call(
        functools.partial(kernel, features, hidden),
        out_shape=(
            jax.ShapeDtypeStruct((RANK, rows_y), f32),
            jax.ShapeDtypeStruct((K - RANK, rows_z), f32),
        ),
        in_specs=[pl.BlockSpec(memory_space=pl.ANY)] * 3,
        out_specs=(pl.BlockSpec(memory_space=pltpu.VMEM), pl.BlockSpec(memory_space=pltpu.VMEM)),
        scratch_shapes=scratch,
        compiler_params=pltpu.CompilerParams(
            collective_id=0, has_side_effects=True, vmem_limit_bytes=58 << 20
        ),
        name="subspace_iteration",
    )(activations, out_grads, sketch)
    return q.T, p.T


def solution(mesh):
    return jax.shard_map(
        body,
        mesh=mesh,
        in_specs=(P("dp", "col"), P("dp", "col"), P("col", None)),
        out_specs=(P(("col", "dp"), None), P(("col", "dp"), None)),
        check_vma=False,
    )
```

```python
import functools

import jax
import jax.numpy as jnp
from jax import lax
from jax.experimental import pallas as pl
from jax.experimental.pallas import tpu as pltpu
from jax.sharding import PartitionSpec as P

RANK = 64
ITERS = 2
K = 128
f32 = jnp.float32
bf16 = jnp.bfloat16
HIGHEST = lax.Precision.HIGHEST
SIDE = 4
HOPS = (2, 1, 3)


def lanes_of(x, k):
    return jnp.broadcast_to(x[:, k : k + 1], (8, K))


def row_of(x, k):
    return jnp.broadcast_to(x[k : k + 1, :], (8, K))


def inverse_factor(matrix):
    lane = lax.broadcasted_iota(jnp.int32, (8, K), 1)
    sub = lax.broadcasted_iota(jnp.int32, (8, K), 0)
    rows = [matrix[8 * u : 8 * u + 8, :] for u in range(16)]
    for b in range(16):
        first = 8 * b
        inside = (lane >= first) & (lane < first + 8)
        pivots = [lanes_of(rows[b], first + k) for k in range(8)]
        panel = jnp.where(inside, jnp.where(lane == sub + first, 1.0, 0.0), rows[b])
        recip, coef, done = [], {}, []
        scale = jnp.zeros((8, K), f32)
        for k in range(8):
            d = row_of(pivots[k], k)
            recip.append(1.0 / d)
            scale = jnp.where(sub == k, lax.rsqrt(d), scale)
            done.append(row_of(panel, k))
            if k < 7:
                c = jnp.where(sub > k, pivots[k] * recip[k], 0.0)
                for m in range(k + 1, 8):
                    coef[k, m] = row_of(pivots[m], k)
                    pivots[m] = pivots[m] - c * coef[k, m]
                panel = panel - c * done[k]
        rows[b] = panel * scale
        for u in range(b + 1, 16):
            cols = [lanes_of(rows[u], first + k) for k in range(8)]
            acc = jnp.where(inside, 0.0, rows[u])
            for k in range(8):
                ck = cols[k] * recip[k]
                for m in range(k + 1, 8):
                    cols[m] = cols[m] - ck * coef[k, m]
                acc = acc - ck * done[k]
            rows[u] = acc
    whole = jnp.concatenate(rows, axis=0)
    i = lax.broadcasted_iota(jnp.int32, (K, K), 0)
    j = lax.broadcasted_iota(jnp.int32, (K, K), 1)
    return jnp.where(j <= i, whole, 0.0)


def wave_rows(rows):
    tiles = rows // 16
    counts = [tiles // 4 + (1 if tiles % 4 > i else 0) for i in (0, 2, 3, 1)]
    spans, first = [], 0
    for count in counts:
        spans.append((first, count * 16))
        first += count * 16
    return (spans[0], spans[1]), (spans[2], spans[3])


def kernel(
    features, hidden, a_hbm, o_hbm, sk_hbm, q_ref, p_ref,
    a, o, sketch, load_sem,
    s_part, s_recv, s_mine, s_all, s_t, s_sem,
    gram_own, gram_first, gram_slots, gram_half, gram_all, gram_sem, factor_y, factor_z,
    *panel_refs,
):
    dp, y = lax.axis_index("dp"), lax.axis_index("col")
    z, x, c = dp // 8, lax.rem(dp // 2, SIDE), lax.rem(dp, 2)
    names = ("own", "c1s", "c1r", "s2", "a2r", "b2r", "s3", "r3", "shard", "gathered", "sem")
    half = len(names)
    bufs_y = dict(zip(names, panel_refs[:half]))
    bufs_z = dict(zip(names, panel_refs[half:]))

    def at(z_=None, x_=None, c_=None):
        z_ = z if z_ is None else z_
        x_ = x if x_ is None else x_
        c_ = c if c_ is None else c_
        return {"dp": (z_ * SIDE + x_) * 2 + c_, "col": y}

    def along(axis, j):
        if axis == "x":
            return at(x_=lax.rem(x + j, SIDE))
        if axis == "z":
            return at(z_=lax.rem(z + j, SIDE))
        if axis == "y":
            return {"dp": dp, "col": lax.rem(y + j, SIDE)}
        return at(c_=1 - c)

    pending = []

    def send(src, dst, sems, index, device):
        copy = pltpu.make_async_remote_copy(
            src_ref=src, dst_ref=dst, send_sem=sems.at[0, index], recv_sem=sems.at[1, index],
            device_id=device, device_id_type=pl.DeviceIdType.MESH,
        )
        copy.start()
        pending.append(copy)
        return copy

    def flush():
        for copy in pending:
            copy.wait_send()
        pending.clear()

    barrier = pltpu.get_barrier_semaphore()
    partners = [along("core", 0)] + [along(axis, j) for axis in "xyz" for j in (1, 2, 3)]
    for device in partners:
        pl.semaphore_signal(barrier, inc=1, device_id=device, device_id_type=pl.DeviceIdType.MESH)

    tokens = s_mine.shape[0]

    def quarter(k, count=1):
        return pl.ds(k * tokens, count * tokens)

    turn = [lax.rem(y + hop, SIDE) for hop in (*HOPS, 0)]
    loads = [pltpu.make_async_copy(sk_hbm, sketch, load_sem.at[0])]
    for held, source, sem in ((o, o_hbm, 1), (a, a_hbm, 5)):
        for k in range(SIDE):
            span = pl.ds(pl.multiple_of(turn[k] * tokens, tokens), tokens)
            loads.append(pltpu.make_async_copy(source.at[span, :], held.at[quarter(k), :], load_sem.at[sem + k]))
    for copy in loads:
        copy.start()

    def send_tokens(k):
        return send(s_part.at[quarter(k), :], s_recv.at[k], s_sem, k, along("y", HOPS[k]))

    def share_tokens(sends, factor):
        total = s_part[quarter(3), :]
        for k in range(3):
            sends[k].wait_recv()
            total = total + s_recv[k]
        if factor is not None:
            total = lax.dot_general(
                total, factor(), (((1,), (1,)), ((), ())), precision=HIGHEST, preferred_element_type=f32
            )
        s_all[quarter(3), :] = total.astype(bf16)
        outs = [
            send(
                s_all.at[quarter(3), :], s_all.at[quarter(HOPS.index(SIDE - hop)), :], s_sem, 3 + k, along("y", hop)
            )
            for k, hop in enumerate(HOPS)
        ]
        s_t[:, quarter(3)] = s_all[quarter(3), :].T
        for copy, hop in zip(outs, HOPS):
            copy.wait_recv()
            came = quarter(HOPS.index(SIDE - hop))
            s_t[:, came] = s_all[came, :].T
        flush()

    def local_gram(bufs, first, count):
        part = bufs["shard"][first : first + count, :]
        return lax.dot_general(
            part, part, (((0,), (0,)), ((), ())), precision=HIGHEST, preferred_element_type=f32
        )

    def gram_steps():
        h = K // 2
        mine = pl.ds(pl.multiple_of(c * h, h), h)
        theirs = pl.ds(pl.multiple_of((1 - c) * h, h), h)
        copy = send(gram_own.at[theirs, :], gram_first, gram_sem, 0, along("core", 0))
        yield
        copy.wait_recv()
        total = gram_own[mine, :] + gram_first[...]
        thirds = ((0, 24, "xzy"), (24, 24, "zyx"), (48, 16, "yxz"))
        places = {"x": x, "z": z, "y": y}
        totals = [total[first : first + count] for first, count, _ in thirds]
        for stage in range(3):
            copies = []
            for part, (first, count, order) in enumerate(thirds):
                span, place = pl.ds(first, count), places[order[stage]]
                gram_slots[stage, place, span, :] = totals[part]
                for j in HOPS:
                    ref = gram_slots.at[stage, place, span, :]
                    copies.append(send(ref, ref, gram_sem, 2 + 9 * stage + 3 * part + j - 1, along(order[stage], j)))
            yield
            for part, (first, count, order) in enumerate(thirds):
                for copy in copies[3 * part : 3 * part + 3]:
                    copy.wait_recv()
                terms = [gram_slots[stage, i, first : first + count, :] for i in range(SIDE)]
                totals[part] = terms[0] + terms[1] + terms[2] + terms[3]
        total = jnp.concatenate(totals, axis=0)
        gram_half[...] = total
        gram_all[mine, :] = total
        copy = send(gram_half, gram_all.at[mine, :], gram_sem, 1, along("core", 0))
        yield
        copy.wait_recv()
        yield

    def factor_from_gram(row_total, out):
        g = gram_all[...]
        i = lax.broadcasted_iota(jnp.int32, (K, K), 0)
        j = lax.broadcasted_iota(jnp.int32, (K, K), 1)
        on_diagonal = jnp.where(i == j, g, 0.0)
        shift = 1e-5 * jnp.sum(jnp.sum(on_diagonal, axis=1, keepdims=True), axis=0, keepdims=True) / K
        out[...] = inverse_factor(g + jnp.where(i == j, shift, 0.0)) * f32(row_total**0.5)

    def pass_panel(weights, bufs, columns, gather):
        own, c1s, c1r, s2, sem = bufs["own"], bufs["c1s"], bufs["c1r"], bufs["s2"], bufs["sem"]
        a2r, b2r, s3, r3, shard, g = bufs["a2r"], bufs["b2r"], bufs["s3"], bufs["r3"], bufs["shard"], bufs["gathered"]
        rows = own.shape[2]
        large = rows > 256
        waves = wave_rows(rows) if large else (((0, rows // 2), (rows // 2, rows // 2)),)
        zs = [lax.rem(z + 1 + k, SIDE) for k in range(SIDE)]
        span = columns // SIDE
        pieces = 1 if span % 1024 == 0 else 2
        first = []

        def compute(k):
            for piece in range(pieces):
                width = span // pieces
                n = SIDE // pieces
                start = pl.multiple_of(zs[k] * span + piece * width, K)
                r = jnp.dot(s_t[...], weights[:, pl.ds(start, width)], preferred_element_type=f32).T
                r = r.reshape(n, 2, rows, K)
                own[k, piece * n : (piece + 1) * n] = jnp.where(c == 0, r[:, 0], r[:, 1])
                c1s[k, piece * n : (piece + 1) * n] = jnp.where(c == 0, r[:, 1], r[:, 0]).astype(bf16)
            first.append(send(c1s.at[k], c1r.at[k], sem, k, along("core", 0)))

        def add_core(k):
            first[k].wait_recv()
            for i in range(SIDE):
                v = own[k, i] + c1r[k, i].astype(f32)
                own[k, i] = v
                s2[k, i] = v.astype(bf16)

        class Wave:
            def __init__(self, index):
                self.a, self.b = waves[index]
                self.base = 4 + 59 * index
                self.second_a, self.second_b, self.third_a, self.third_b = [], [], [], []
                self.gather_a, self.gather_b, self.on_a, self.on_b, self.cores = [], [], {}, {}, []

            def second(self, k):
                for j in (1, 2, 3):
                    there = lax.rem(x + j, SIDE)
                    self.second_a.append(
                        send(
                            s2.at[k, there, pl.ds(*self.a), :], a2r.at[k, j - 1, pl.ds(*self.a), :],
                            sem, self.base + k * 3 + j - 1, along("x", j),
                        )
                    )
                if k < 3:
                    self.second_b.append(
                        send(
                            s2.at[k, :, pl.ds(*self.b), :], b2r.at[k, :, pl.ds(*self.b), :],
                            sem, self.base + 12 + k, along("z", k + 1),
                        )
                    )

            def third(self):
                part = pl.ds(*self.a)
                for k in range(SIDE):
                    total = own[k, x, part, :]
                    for j in range(3):
                        self.second_a[k * 3 + j].wait_recv()
                        total = total + a2r[k, j, part, :].astype(f32)
                    if k < 3:
                        s3[k, part, :] = total.astype(bf16)
                        self.third_a.append(
                            send(s3.at[k, part, :], r3.at[k, part, :], sem, self.base + 15 + k, along("z", k + 1))
                        )
                    else:
                        shard[part, :] = total
                part = pl.ds(*self.b)
                for k in range(3):
                    self.second_b[k].wait_recv()
                for k in range(SIDE):
                    there = lax.rem(x + 1 + k, SIDE)
                    total = own[3, there, part, :]
                    for j in range(3):
                        total = total + b2r[j, there, part, :].astype(f32)
                    if k < 3:
                        s3[k, part, :] = total.astype(bf16)
                        self.third_b.append(
                            send(s3.at[k, part, :], r3.at[k, part, :], sem, self.base + 18 + k, along("x", k + 1))
                        )
                    else:
                        shard[part, :] = total

            def piece(self, z_, x_, part):
                return g.at[z_, x_, c, pl.ds(*part), :]

            def finish(self):
                for part, copies in ((self.a, self.third_a), (self.b, self.third_b)):
                    part = pl.ds(*part)
                    total = shard[part, :]
                    for k in range(3):
                        copies[k].wait_recv()
                        total = total + r3[k, part, :].astype(f32)
                    shard[part, :] = total
                    if gather:
                        g[z, x, c, part, :] = total.astype(bf16)
                        axis, part, base, outs = (
                            ("z", self.a, 21, self.gather_a) if copies is self.third_a else ("x", self.b, 24, self.gather_b)
                        )
                        for j in (1, 2, 3):
                            ref = self.piece(z, x, part)
                            outs.append(send(ref, ref, sem, self.base + base + j - 1, along(axis, j)))
                if gather:
                    self.forward(0)

            def forward(self, k):
                if k > 0:
                    self.gather_a[k - 1].wait_recv()
                    self.gather_b[k - 1].wait_recv()
                from_z, from_x = lax.rem(z - k + SIDE, SIDE), lax.rem(x - k + SIDE, SIDE)
                for j in (1, 2, 3):
                    ref = self.piece(from_z, x, self.a)
                    self.on_a[k, j] = send(ref, ref, sem, self.base + 27 + k * 3 + j - 1, along("x", j))
                    ref = self.piece(z, from_x, self.b)
                    self.on_b[k, j] = send(ref, ref, sem, self.base + 39 + k * 3 + j - 1, along("z", j))

            def over(self, ref):
                self.cores.append(send(ref, ref, sem, self.base + 51 + len(self.cores), along("core", 0)))

            def first_hop(self):
                for k in (1, 2, 3):
                    self.forward(k)
                self.over(g.at[:, x, c, pl.ds(*self.a), :])
                self.over(g.at[z, :, c, pl.ds(*self.b), :])

            def second_hop(self):
                for j in (1, 2, 3):
                    for k in range(SIDE):
                        self.on_a[k, j].wait_recv()
                    self.over(g.at[:, lax.rem(x - j + SIDE, SIDE), c, pl.ds(*self.a), :])
                    for k in range(SIDE):
                        self.on_b[k, j].wait_recv()
                    self.over(g.at[lax.rem(z - j + SIDE, SIDE), :, c, pl.ds(*self.b), :])

            def wait_cores(self):
                for copy in self.cores:
                    copy.wait_recv()

        parts = [Wave(index) for index in range(len(waves))]
        one, two = parts[0], parts[-1]
        for k in range(SIDE):
            compute(k)
            if k > 0:
                add_core(k - 1)
                one.second(k - 1)
        add_core(3)
        one.second(3)
        if large:
            for k in range(SIDE):
                two.second(k)
            one.third()
        two.third()
        if large:
            one.finish()
            first, count = one.a[0], one.a[1] + one.b[1]
            gram_own[...] = local_gram(bufs, first, count)
            two.finish()
            gram_own[...] += local_gram(bufs, first + count, rows - count)
        else:
            two.finish()
            gram_own[...] = local_gram(bufs, 0, rows)
        steps = gram_steps()
        if not gather:
            return steps
        next(steps)
        next(steps)
        for wave in parts:
            wave.first_hop()
        next(steps)
        for wave in parts:
            wave.second_hop()
        next(steps)
        for wave in parts:
            wave.wait_cores()
        return steps

    row_y, row_z = float(SIDE * features), float(SIDE * hidden)
    for iteration in range(ITERS):
        sends = []
        if iteration == 0:
            loads[0].wait()
            for k, count in ((0, 2), (2, 1), (3, 1)):
                for n in range(k, k + count):
                    loads[1 + n].wait()
                s_part[quarter(k, count), :] = jnp.zeros((count * tokens, K), f32)

                @pl.loop(0, 2)
                def _(i):
                    deep = pl.ds(pl.multiple_of(i * (hidden // 2), K), hidden // 2)
                    s_part[quarter(k, count), :] += jnp.dot(
                        o[quarter(k, count), deep], sketch[deep, :], preferred_element_type=f32
                    )

                if k == 0:
                    pl.semaphore_wait(barrier, len(partners))
                if k < 3:
                    sends += [send_tokens(n) for n in range(k, k + count)]
            for k in range(SIDE):
                loads[5 + k].wait()
            share_tokens(sends, None)
        else:
            s_part[...] = jnp.zeros(s_part.shape, f32)
            n = hidden // 2

            @pl.loop(0, 2)
            def _(i):
                deep = pl.ds(pl.multiple_of(i * n, K), n)
                block = bufs_z["gathered"][pl.ds(2 * i, 2)].reshape(n, K)
                s_part[...] += jnp.dot(o[:, deep], block, preferred_element_type=f32)

            sends = [send_tokens(k) for k in range(3)]
            for _ in steps:
                pass
            factor_from_gram(row_z, factor_z)
            share_tokens(sends, lambda: factor_z[...])
        steps = pass_panel(a, bufs_y, features, True)
        s_part[...] = jnp.dot(a[...], bufs_y["gathered"][...].reshape(features, K), preferred_element_type=f32)
        sends = [send_tokens(k) for k in range(3)]
        for _ in steps:
            pass
        factor_from_gram(row_y, factor_y)
        share_tokens(sends, lambda: factor_y[...])
        if iteration == ITERS - 1:
            q = lax.dot_general(
                factor_y[...], bufs_y["shard"][...], (((1,), (1,)), ((), ())), precision=HIGHEST, preferred_element_type=f32
            )
            q_ref[...] = q[:RANK, :]
        steps = pass_panel(o, bufs_z, hidden, iteration < ITERS - 1)
    for _ in steps:
        pass
    factor_from_gram(row_z, factor_z)
    p = lax.dot_general(
        factor_z[...], bufs_z["shard"][...], (((1,), (1,)), ((), ())), precision=HIGHEST, preferred_element_type=f32
    )
    p_ref[...] = p[RANK:, :]
    flush()


def copy_out(q_ref, p_ref, q_out, p_out):
    q_out[...] = q_ref[...]
    p_out[...] = p_ref[...]


def panel_scratch(rows):
    return [
        pltpu.VMEM((4, 4, rows, K), f32),
        pltpu.VMEM((4, 4, rows, K), bf16),
        pltpu.VMEM((4, 4, rows, K), bf16),
        pltpu.VMEM((4, 4, rows, K), bf16),
        pltpu.VMEM((4, 3, rows, K), bf16),
        pltpu.VMEM((3, 4, rows, K), bf16),
        pltpu.VMEM((3, rows, K), bf16),
        pltpu.VMEM((3, rows, K), bf16),
        pltpu.VMEM((rows, K), f32),
        pltpu.VMEM((4, 4, 2, rows, K), bf16),
        pltpu.SemaphoreType.DMA((2, 122)),
    ]


def body(activations, out_grads, sketch):
    tokens, features = activations.shape
    hidden = out_grads.shape[1]
    devices = lax.axis_size("dp")
    rows_y, rows_z = features // devices, hidden // devices
    quarter = tokens // SIDE
    scratch = [
        pltpu.VMEM((tokens, features), bf16),
        pltpu.VMEM((tokens, hidden), bf16),
        pltpu.VMEM((hidden, K), bf16),
        pltpu.SemaphoreType.DMA((9,)),
        pltpu.VMEM((tokens, K), f32),
        pltpu.VMEM((3, quarter, K), f32),
        pltpu.VMEM((quarter, K), bf16),
        pltpu.VMEM((tokens, K), bf16),
        pltpu.VMEM((K, tokens), bf16),
        pltpu.SemaphoreType.DMA((2, 6)),
        pltpu.VMEM((K, K), f32),
        pltpu.VMEM((K // 2, K), f32),
        pltpu.VMEM((3, SIDE, K // 2, K), f32),
        pltpu.VMEM((K // 2, K), f32),
        pltpu.VMEM((K, K), f32),
        pltpu.SemaphoreType.DMA((2, 29)),
        pltpu.VMEM((K, K), f32),
        pltpu.VMEM((K, K), f32),
        *panel_scratch(rows_y),
        *panel_scratch(rows_z),
    ]
    q, p = pl.pallas_call(
        functools.partial(kernel, features, hidden),
        out_shape=(
            jax.ShapeDtypeStruct((RANK, rows_y), f32),
            jax.ShapeDtypeStruct((K - RANK, rows_z), f32),
        ),
        in_specs=[pl.BlockSpec(memory_space=pl.ANY)] * 3,
        out_specs=(pl.BlockSpec(memory_space=pltpu.VMEM), pl.BlockSpec(memory_space=pltpu.VMEM)),
        scratch_shapes=scratch,
        compiler_params=pltpu.CompilerParams(
            collective_id=0, has_side_effects=True, vmem_limit_bytes=58 << 20
        ),
        name="subspace_iteration",
    )(activations, out_grads, sketch)
    q, p = pl.pallas_call(
        copy_out,
        out_shape=(jax.ShapeDtypeStruct(q.shape, f32), jax.ShapeDtypeStruct(p.shape, f32)),
        in_specs=[pl.BlockSpec(memory_space=pltpu.VMEM)] * 2,
        out_specs=(pl.BlockSpec(memory_space=pltpu.VMEM), pl.BlockSpec(memory_space=pltpu.VMEM)),
        name="write_outputs",
    )(q, p)
    return q.T, p.T


def solution(mesh):
    return jax.shard_map(
        body,
        mesh=mesh,
        in_specs=(P("dp", "col"), P("dp", "col"), P("col", None)),
        out_specs=(P(("col", "dp"), None), P(("col", "dp"), None)),
        check_vma=False,
    )
```

```python
import functools

import jax
import jax.numpy as jnp
from jax import lax
from jax.experimental import pallas as pl
from jax.experimental.pallas import tpu as pltpu
from jax.sharding import PartitionSpec as P

RANK = 64
ITERS = 2
K = 128
f32 = jnp.float32
bf16 = jnp.bfloat16
HIGHEST = lax.Precision.HIGHEST
SIDE = 4
HOPS = (2, 1, 3)


def lanes_of(x, k):
    return jnp.broadcast_to(x[:, k : k + 1], (8, K))


def row_of(x, k):
    return jnp.broadcast_to(x[k : k + 1, :], (8, K))


def inverse_factor(matrix):
    lane = lax.broadcasted_iota(jnp.int32, (8, K), 1)
    sub = lax.broadcasted_iota(jnp.int32, (8, K), 0)
    rows = [matrix[8 * u : 8 * u + 8, :] for u in range(16)]
    for b in range(16):
        first = 8 * b
        inside = (lane >= first) & (lane < first + 8)
        pivots = [lanes_of(rows[b], first + k) for k in range(8)]
        panel = jnp.where(inside, jnp.where(lane == sub + first, 1.0, 0.0), rows[b])
        recip, coef, done = [], {}, []
        scale = jnp.zeros((8, K), f32)
        for k in range(8):
            d = row_of(pivots[k], k)
            recip.append(1.0 / d)
            scale = jnp.where(sub == k, lax.rsqrt(d), scale)
            done.append(row_of(panel, k))
            if k < 7:
                c = jnp.where(sub > k, pivots[k] * recip[k], 0.0)
                for m in range(k + 1, 8):
                    coef[k, m] = row_of(pivots[m], k)
                    pivots[m] = pivots[m] - c * coef[k, m]
                panel = panel - c * done[k]
        rows[b] = panel * scale
        for u in range(b + 1, 16):
            cols = [lanes_of(rows[u], first + k) for k in range(8)]
            acc = jnp.where(inside, 0.0, rows[u])
            for k in range(8):
                ck = cols[k] * recip[k]
                for m in range(k + 1, 8):
                    cols[m] = cols[m] - ck * coef[k, m]
                acc = acc - ck * done[k]
            rows[u] = acc
    whole = jnp.concatenate(rows, axis=0)
    i = lax.broadcasted_iota(jnp.int32, (K, K), 0)
    j = lax.broadcasted_iota(jnp.int32, (K, K), 1)
    return jnp.where(j <= i, whole, 0.0)


def wave_rows(rows):
    tiles = rows // 16
    counts = [tiles // 4 + (1 if tiles % 4 > i else 0) for i in (0, 2, 3, 1)]
    spans, first = [], 0
    for count in counts:
        spans.append((first, count * 16))
        first += count * 16
    return (spans[0], spans[1]), (spans[2], spans[3])


def kernel(
    features, hidden, a_hbm, o_hbm, sk_hbm, q_ref, p_ref,
    a, o, sketch, load_sem,
    s_part, s_recv, s_mine, s_all, s_t, s_sem,
    gram_own, gram_first, gram_slots, gram_half, gram_all, gram_sem, factor_y, factor_z,
    *panel_refs,
):
    dp, y = lax.axis_index("dp"), lax.axis_index("col")
    z, x, c = dp // 8, lax.rem(dp // 2, SIDE), lax.rem(dp, 2)
    names = ("own", "c1s", "c1r", "s2", "a2r", "b2r", "s3", "r3", "shard", "gathered", "sem")
    half = len(names)
    bufs_y = dict(zip(names, panel_refs[:half]))
    bufs_z = dict(zip(names, panel_refs[half:]))

    def at(z_=None, x_=None, c_=None):
        z_ = z if z_ is None else z_
        x_ = x if x_ is None else x_
        c_ = c if c_ is None else c_
        return {"dp": (z_ * SIDE + x_) * 2 + c_, "col": y}

    def along(axis, j):
        if axis == "x":
            return at(x_=lax.rem(x + j, SIDE))
        if axis == "z":
            return at(z_=lax.rem(z + j, SIDE))
        if axis == "y":
            return {"dp": dp, "col": lax.rem(y + j, SIDE)}
        return at(c_=1 - c)

    pending = []

    def send(src, dst, sems, index, device):
        copy = pltpu.make_async_remote_copy(
            src_ref=src, dst_ref=dst, send_sem=sems.at[0, index], recv_sem=sems.at[1, index],
            device_id=device, device_id_type=pl.DeviceIdType.MESH,
        )
        copy.start()
        pending.append(copy)
        return copy

    def flush():
        for copy in pending:
            copy.wait_send()
        pending.clear()

    barrier = pltpu.get_barrier_semaphore()
    partners = [along("core", 0)] + [along(axis, j) for axis in "xyz" for j in (1, 2, 3)]
    for device in partners:
        pl.semaphore_signal(barrier, inc=1, device_id=device, device_id_type=pl.DeviceIdType.MESH)

    tokens = s_mine.shape[0]
    turn = [lax.rem(y + hop, SIDE) for hop in (*HOPS, 0)]
    loads = [pltpu.make_async_copy(sk_hbm, sketch, load_sem.at[0])]
    for k in range(SIDE):
        span = pl.ds(pl.multiple_of(turn[k] * tokens, tokens), tokens)
        loads.append(pltpu.make_async_copy(o_hbm.at[span, :], o.at[span, :], load_sem.at[1 + k]))
    loads.append(pltpu.make_async_copy(a_hbm, a, load_sem.at[5]))
    for copy in loads:
        copy.start()

    def send_tokens(k):
        span = pl.ds(pl.multiple_of(turn[k] * tokens, tokens), tokens)
        return send(s_part.at[span, :], s_recv.at[k], s_sem, k, along("y", HOPS[k]))

    def share_tokens(sends, factor):
        span = pl.ds(pl.multiple_of(y * tokens, tokens), tokens)
        total = s_part[span, :]
        for k in range(3):
            sends[k].wait_recv()
            total = total + s_recv[k]
        if factor is not None:
            total = lax.dot_general(
                total, factor(), (((1,), (1,)), ((), ())), precision=HIGHEST, preferred_element_type=f32
            )
        s_all[span, :] = total.astype(bf16)
        outs = [send(s_all.at[span, :], s_all.at[span, :], s_sem, 3 + k, along("y", HOPS[k])) for k in range(3)]
        for copy in outs:
            copy.wait_recv()
        flush()
        s_t[...] = s_all[...].T

    def local_gram(bufs, first, count):
        part = bufs["shard"][first : first + count, :]
        return lax.dot_general(
            part, part, (((0,), (0,)), ((), ())), precision=HIGHEST, preferred_element_type=f32
        )

    def gram_steps():
        h = K // 2
        mine = pl.ds(pl.multiple_of(c * h, h), h)
        theirs = pl.ds(pl.multiple_of((1 - c) * h, h), h)
        copy = send(gram_own.at[theirs, :], gram_first, gram_sem, 0, along("core", 0))
        yield
        copy.wait_recv()
        total = gram_own[mine, :] + gram_first[...]
        thirds = ((0, 24, "xzy"), (24, 24, "zyx"), (48, 16, "yxz"))
        places = {"x": x, "z": z, "y": y}
        totals = [total[first : first + count] for first, count, _ in thirds]
        for stage in range(3):
            copies = []
            for part, (first, count, order) in enumerate(thirds):
                span, place = pl.ds(first, count), places[order[stage]]
                gram_slots[stage, place, span, :] = totals[part]
                for j in HOPS:
                    ref = gram_slots.at[stage, place, span, :]
                    copies.append(send(ref, ref, gram_sem, 2 + 9 * stage + 3 * part + j - 1, along(order[stage], j)))
            yield
            for part, (first, count, order) in enumerate(thirds):
                for copy in copies[3 * part : 3 * part + 3]:
                    copy.wait_recv()
                terms = [gram_slots[stage, i, first : first + count, :] for i in range(SIDE)]
                totals[part] = terms[0] + terms[1] + terms[2] + terms[3]
        total = jnp.concatenate(totals, axis=0)
        gram_half[...] = total
        gram_all[mine, :] = total
        copy = send(gram_half, gram_all.at[mine, :], gram_sem, 1, along("core", 0))
        yield
        copy.wait_recv()
        yield

    def factor_from_gram(row_total, out):
        g = gram_all[...]
        i = lax.broadcasted_iota(jnp.int32, (K, K), 0)
        j = lax.broadcasted_iota(jnp.int32, (K, K), 1)
        on_diagonal = jnp.where(i == j, g, 0.0)
        shift = 1e-5 * jnp.sum(jnp.sum(on_diagonal, axis=1, keepdims=True), axis=0, keepdims=True) / K
        out[...] = inverse_factor(g + jnp.where(i == j, shift, 0.0)) * f32(row_total**0.5)

    def pass_panel(weights, bufs, columns, gather):
        own, c1s, c1r, s2, sem = bufs["own"], bufs["c1s"], bufs["c1r"], bufs["s2"], bufs["sem"]
        a2r, b2r, s3, r3, shard, g = bufs["a2r"], bufs["b2r"], bufs["s3"], bufs["r3"], bufs["shard"], bufs["gathered"]
        rows = own.shape[2]
        large = rows > 256
        waves = wave_rows(rows) if large else (((0, rows // 2), (rows // 2, rows // 2)),)
        zs = [lax.rem(z + 1 + k, SIDE) for k in range(SIDE)]
        span = columns // SIDE
        pieces = 1 if span % 1024 == 0 else 2
        first = []

        def compute(k):
            for piece in range(pieces):
                width = span // pieces
                n = SIDE // pieces
                start = pl.multiple_of(zs[k] * span + piece * width, K)
                r = jnp.dot(s_t[...], weights[:, pl.ds(start, width)], preferred_element_type=f32).T
                r = r.reshape(n, 2, rows, K)
                own[k, piece * n : (piece + 1) * n] = jnp.where(c == 0, r[:, 0], r[:, 1])
                c1s[k, piece * n : (piece + 1) * n] = jnp.where(c == 0, r[:, 1], r[:, 0]).astype(bf16)
            first.append(send(c1s.at[k], c1r.at[k], sem, k, along("core", 0)))

        def add_core(k):
            first[k].wait_recv()
            for i in range(SIDE):
                v = own[k, i] + c1r[k, i].astype(f32)
                own[k, i] = v
                s2[k, i] = v.astype(bf16)

        class Wave:
            def __init__(self, index):
                self.a, self.b = waves[index]
                self.base = 4 + 59 * index
                self.second_a, self.second_b, self.third_a, self.third_b = [], [], [], []
                self.gather_a, self.gather_b, self.on_a, self.on_b, self.cores = [], [], {}, {}, []

            def second(self, k):
                for j in (1, 2, 3):
                    there = lax.rem(x + j, SIDE)
                    self.second_a.append(
                        send(
                            s2.at[k, there, pl.ds(*self.a), :], a2r.at[k, j - 1, pl.ds(*self.a), :],
                            sem, self.base + k * 3 + j - 1, along("x", j),
                        )
                    )
                if k < 3:
                    self.second_b.append(
                        send(
                            s2.at[k, :, pl.ds(*self.b), :], b2r.at[k, :, pl.ds(*self.b), :],
                            sem, self.base + 12 + k, along("z", k + 1),
                        )
                    )

            def third(self):
                part = pl.ds(*self.a)
                for k in range(SIDE):
                    total = own[k, x, part, :]
                    for j in range(3):
                        self.second_a[k * 3 + j].wait_recv()
                        total = total + a2r[k, j, part, :].astype(f32)
                    if k < 3:
                        s3[k, part, :] = total.astype(bf16)
                        self.third_a.append(
                            send(s3.at[k, part, :], r3.at[k, part, :], sem, self.base + 15 + k, along("z", k + 1))
                        )
                    else:
                        shard[part, :] = total
                part = pl.ds(*self.b)
                for k in range(3):
                    self.second_b[k].wait_recv()
                for k in range(SIDE):
                    there = lax.rem(x + 1 + k, SIDE)
                    total = own[3, there, part, :]
                    for j in range(3):
                        total = total + b2r[j, there, part, :].astype(f32)
                    if k < 3:
                        s3[k, part, :] = total.astype(bf16)
                        self.third_b.append(
                            send(s3.at[k, part, :], r3.at[k, part, :], sem, self.base + 18 + k, along("x", k + 1))
                        )
                    else:
                        shard[part, :] = total

            def piece(self, z_, x_, part):
                return g.at[z_, x_, c, pl.ds(*part), :]

            def finish(self):
                for part, copies in ((self.a, self.third_a), (self.b, self.third_b)):
                    part = pl.ds(*part)
                    total = shard[part, :]
                    for k in range(3):
                        copies[k].wait_recv()
                        total = total + r3[k, part, :].astype(f32)
                    shard[part, :] = total
                    if gather:
                        g[z, x, c, part, :] = total.astype(bf16)
                        axis, part, base, outs = (
                            ("z", self.a, 21, self.gather_a) if copies is self.third_a else ("x", self.b, 24, self.gather_b)
                        )
                        for j in (1, 2, 3):
                            ref = self.piece(z, x, part)
                            outs.append(send(ref, ref, sem, self.base + base + j - 1, along(axis, j)))
                if gather:
                    self.forward(0)

            def forward(self, k):
                if k > 0:
                    self.gather_a[k - 1].wait_recv()
                    self.gather_b[k - 1].wait_recv()
                from_z, from_x = lax.rem(z - k + SIDE, SIDE), lax.rem(x - k + SIDE, SIDE)
                for j in (1, 2, 3):
                    ref = self.piece(from_z, x, self.a)
                    self.on_a[k, j] = send(ref, ref, sem, self.base + 27 + k * 3 + j - 1, along("x", j))
                    ref = self.piece(z, from_x, self.b)
                    self.on_b[k, j] = send(ref, ref, sem, self.base + 39 + k * 3 + j - 1, along("z", j))

            def over(self, ref):
                self.cores.append(send(ref, ref, sem, self.base + 51 + len(self.cores), along("core", 0)))

            def first_hop(self):
                for k in (1, 2, 3):
                    self.forward(k)
                self.over(g.at[:, x, c, pl.ds(*self.a), :])
                self.over(g.at[z, :, c, pl.ds(*self.b), :])

            def second_hop(self):
                for j in (1, 2, 3):
                    for k in range(SIDE):
                        self.on_a[k, j].wait_recv()
                    self.over(g.at[:, lax.rem(x - j + SIDE, SIDE), c, pl.ds(*self.a), :])
                    for k in range(SIDE):
                        self.on_b[k, j].wait_recv()
                    self.over(g.at[lax.rem(z - j + SIDE, SIDE), :, c, pl.ds(*self.b), :])

            def wait_cores(self):
                for copy in self.cores:
                    copy.wait_recv()

        parts = [Wave(index) for index in range(len(waves))]
        one, two = parts[0], parts[-1]
        for k in range(SIDE):
            compute(k)
            if k > 0:
                add_core(k - 1)
                one.second(k - 1)
        add_core(3)
        one.second(3)
        if large:
            for k in range(SIDE):
                two.second(k)
            one.third()
        two.third()
        if large:
            one.finish()
            first, count = one.a[0], one.a[1] + one.b[1]
            gram_own[...] = local_gram(bufs, first, count)
            two.finish()
            gram_own[...] += local_gram(bufs, first + count, rows - count)
        else:
            two.finish()
            gram_own[...] = local_gram(bufs, 0, rows)
        steps = gram_steps()
        if not gather:
            return steps
        next(steps)
        next(steps)
        for wave in parts:
            wave.first_hop()
        next(steps)
        for wave in parts:
            wave.second_hop()
        next(steps)
        for wave in parts:
            wave.wait_cores()
        return steps

    row_y, row_z = float(SIDE * features), float(SIDE * hidden)
    for iteration in range(ITERS):
        sends = []
        if iteration == 0:
            loads[0].wait()
            for k in range(SIDE):
                span = pl.ds(pl.multiple_of(turn[k] * tokens, tokens), tokens)
                loads[1 + k].wait()
                s_part[span, :] = jnp.zeros((tokens, K), f32)

                @pl.loop(0, SIDE)
                def _(i):
                    deep = pl.ds(pl.multiple_of(i * (hidden // SIDE), K), hidden // SIDE)
                    s_part[span, :] += jnp.dot(o[span, deep], sketch[deep, :], preferred_element_type=f32)

                if k == 0:
                    pl.semaphore_wait(barrier, len(partners))
                if k < 3:
                    sends.append(send_tokens(k))
            loads[5].wait()
            share_tokens(sends, None)
        else:
            s_part[...] = jnp.zeros(s_part.shape, f32)
            n = hidden // SIDE

            @pl.loop(0, SIDE)
            def _(i):
                deep = pl.ds(pl.multiple_of(i * n, K), n)
                block = bufs_z["gathered"][i].reshape(n, K)
                s_part[...] += jnp.dot(o[:, deep], block, preferred_element_type=f32)

            sends = [send_tokens(k) for k in range(3)]
            for _ in steps:
                pass
            factor_from_gram(row_z, factor_z)
            share_tokens(sends, lambda: factor_z[...])
        steps = pass_panel(a, bufs_y, features, True)
        s_part[...] = jnp.dot(a[...], bufs_y["gathered"][...].reshape(features, K), preferred_element_type=f32)
        sends = [send_tokens(k) for k in range(3)]
        for _ in steps:
            pass
        factor_from_gram(row_y, factor_y)
        share_tokens(sends, lambda: factor_y[...])
        if iteration == ITERS - 1:
            q = lax.dot_general(
                factor_y[...], bufs_y["shard"][...], (((1,), (1,)), ((), ())), precision=HIGHEST, preferred_element_type=f32
            )
            q_ref[...] = q[:RANK, :]
        steps = pass_panel(o, bufs_z, hidden, iteration < ITERS - 1)
    for _ in steps:
        pass
    factor_from_gram(row_z, factor_z)
    p = lax.dot_general(
        factor_z[...], bufs_z["shard"][...], (((1,), (1,)), ((), ())), precision=HIGHEST, preferred_element_type=f32
    )
    p_ref[...] = p[RANK:, :]
    flush()


def copy_out(q_ref, p_ref, q_out, p_out):
    q_out[...] = q_ref[...]
    p_out[...] = p_ref[...]


def panel_scratch(rows):
    return [
        pltpu.VMEM((4, 4, rows, K), f32),
        pltpu.VMEM((4, 4, rows, K), bf16),
        pltpu.VMEM((4, 4, rows, K), bf16),
        pltpu.VMEM((4, 4, rows, K), bf16),
        pltpu.VMEM((4, 3, rows, K), bf16),
        pltpu.VMEM((3, 4, rows, K), bf16),
        pltpu.VMEM((3, rows, K), bf16),
        pltpu.VMEM((3, rows, K), bf16),
        pltpu.VMEM((rows, K), f32),
        pltpu.VMEM((4, 4, 2, rows, K), bf16),
        pltpu.SemaphoreType.DMA((2, 122)),
    ]


def body(activations, out_grads, sketch):
    tokens, features = activations.shape
    hidden = out_grads.shape[1]
    devices = lax.axis_size("dp")
    rows_y, rows_z = features // devices, hidden // devices
    quarter = tokens // SIDE
    scratch = [
        pltpu.VMEM((tokens, features), bf16),
        pltpu.VMEM((tokens, hidden), bf16),
        pltpu.VMEM((hidden, K), bf16),
        pltpu.SemaphoreType.DMA((6,)),
        pltpu.VMEM((tokens, K), f32),
        pltpu.VMEM((3, quarter, K), f32),
        pltpu.VMEM((quarter, K), bf16),
        pltpu.VMEM((tokens, K), bf16),
        pltpu.VMEM((K, tokens), bf16),
        pltpu.SemaphoreType.DMA((2, 6)),
        pltpu.VMEM((K, K), f32),
        pltpu.VMEM((K // 2, K), f32),
        pltpu.VMEM((3, SIDE, K // 2, K), f32),
        pltpu.VMEM((K // 2, K), f32),
        pltpu.VMEM((K, K), f32),
        pltpu.SemaphoreType.DMA((2, 29)),
        pltpu.VMEM((K, K), f32),
        pltpu.VMEM((K, K), f32),
        *panel_scratch(rows_y),
        *panel_scratch(rows_z),
    ]
    q, p = pl.pallas_call(
        functools.partial(kernel, features, hidden),
        out_shape=(
            jax.ShapeDtypeStruct((RANK, rows_y), f32),
            jax.ShapeDtypeStruct((K - RANK, rows_z), f32),
        ),
        in_specs=[pl.BlockSpec(memory_space=pl.ANY)] * 3,
        out_specs=(pl.BlockSpec(memory_space=pltpu.VMEM), pl.BlockSpec(memory_space=pltpu.VMEM)),
        scratch_shapes=scratch,
        compiler_params=pltpu.CompilerParams(
            collective_id=0, has_side_effects=True, vmem_limit_bytes=58 << 20
        ),
        name="subspace_iteration",
    )(activations, out_grads, sketch)
    q, p = pl.pallas_call(
        copy_out,
        out_shape=(jax.ShapeDtypeStruct(q.shape, f32), jax.ShapeDtypeStruct(p.shape, f32)),
        in_specs=[pl.BlockSpec(memory_space=pltpu.VMEM)] * 2,
        out_specs=(pl.BlockSpec(memory_space=pltpu.VMEM), pl.BlockSpec(memory_space=pltpu.VMEM)),
        name="write_outputs",
    )(q, p)
    return q.T, p.T


def solution(mesh):
    return jax.shard_map(
        body,
        mesh=mesh,
        in_specs=(P("dp", "col"), P("dp", "col"), P("col", None)),
        out_specs=(P(("col", "dp"), None), P(("col", "dp"), None)),
        check_vma=False,
    )
```

```python
import functools

import jax
import jax.numpy as jnp
from jax import lax
from jax.experimental import pallas as pl
from jax.experimental.pallas import tpu as pltpu
from jax.sharding import PartitionSpec as P

RANK = 64
ITERS = 2
K = 128
f32 = jnp.float32
bf16 = jnp.bfloat16
HIGHEST = lax.Precision.HIGHEST
SIDE = 4
HOPS = (2, 1, 3)


def lanes_of(x, k):
    return jnp.broadcast_to(x[:, k : k + 1], (8, K))


def row_of(x, k):
    return jnp.broadcast_to(x[k : k + 1, :], (8, K))


def inverse_factor(matrix):
    lane = lax.broadcasted_iota(jnp.int32, (8, K), 1)
    sub = lax.broadcasted_iota(jnp.int32, (8, K), 0)
    rows = [matrix[8 * u : 8 * u + 8, :] for u in range(16)]
    for b in range(16):
        first = 8 * b
        inside = (lane >= first) & (lane < first + 8)
        pivots = [lanes_of(rows[b], first + k) for k in range(8)]
        panel = jnp.where(inside, jnp.where(lane == sub + first, 1.0, 0.0), rows[b])
        recip, coef, done = [], {}, []
        scale = jnp.zeros((8, K), f32)
        for k in range(8):
            d = row_of(pivots[k], k)
            recip.append(1.0 / d)
            scale = jnp.where(sub == k, lax.rsqrt(d), scale)
            done.append(row_of(panel, k))
            if k < 7:
                c = jnp.where(sub > k, pivots[k] * recip[k], 0.0)
                for m in range(k + 1, 8):
                    coef[k, m] = row_of(pivots[m], k)
                    pivots[m] = pivots[m] - c * coef[k, m]
                panel = panel - c * done[k]
        rows[b] = panel * scale
        for u in range(b + 1, 16):
            cols = [lanes_of(rows[u], first + k) for k in range(8)]
            acc = jnp.where(inside, 0.0, rows[u])
            for k in range(8):
                ck = cols[k] * recip[k]
                for m in range(k + 1, 8):
                    cols[m] = cols[m] - ck * coef[k, m]
                acc = acc - ck * done[k]
            rows[u] = acc
    whole = jnp.concatenate(rows, axis=0)
    i = lax.broadcasted_iota(jnp.int32, (K, K), 0)
    j = lax.broadcasted_iota(jnp.int32, (K, K), 1)
    return jnp.where(j <= i, whole, 0.0)


def wave_rows(rows):
    tiles = rows // 16
    counts = [tiles // 4 + (1 if tiles % 4 > i else 0) for i in (0, 2, 3, 1)]
    spans, first = [], 0
    for count in counts:
        spans.append((first, count * 16))
        first += count * 16
    return (spans[0], spans[1]), (spans[2], spans[3])


def kernel(
    features, hidden, a_hbm, o_hbm, sk_hbm, q_ref, p_ref,
    a, o, sketch, load_sem,
    s_part, s_recv, s_mine, s_all, s_t, s_sem,
    gram_own, gram_first, gram_slots, gram_half, gram_all, gram_sem, factor_y, factor_z,
    *panel_refs,
):
    dp, y = lax.axis_index("dp"), lax.axis_index("col")
    z, x, c = dp // 8, lax.rem(dp // 2, SIDE), lax.rem(dp, 2)
    names = ("own", "c1s", "c1r", "s2", "a2r", "b2r", "s3", "r3", "shard", "gathered", "sem")
    half = len(names)
    bufs_y = dict(zip(names, panel_refs[:half]))
    bufs_z = dict(zip(names, panel_refs[half:]))

    def at(z_=None, x_=None, c_=None):
        z_ = z if z_ is None else z_
        x_ = x if x_ is None else x_
        c_ = c if c_ is None else c_
        return {"dp": (z_ * SIDE + x_) * 2 + c_, "col": y}

    def along(axis, j):
        if axis == "x":
            return at(x_=lax.rem(x + j, SIDE))
        if axis == "z":
            return at(z_=lax.rem(z + j, SIDE))
        if axis == "y":
            return {"dp": dp, "col": lax.rem(y + j, SIDE)}
        return at(c_=1 - c)

    pending = []

    def send(src, dst, sems, index, device):
        copy = pltpu.make_async_remote_copy(
            src_ref=src, dst_ref=dst, send_sem=sems.at[0, index], recv_sem=sems.at[1, index],
            device_id=device, device_id_type=pl.DeviceIdType.MESH,
        )
        copy.start()
        pending.append(copy)
        return copy

    def flush():
        for copy in pending:
            copy.wait_send()
        pending.clear()

    barrier = pltpu.get_barrier_semaphore()
    partners = [along("core", 0)] + [along(axis, j) for axis in "xyz" for j in (1, 2, 3)]
    for device in partners:
        pl.semaphore_signal(barrier, inc=1, device_id=device, device_id_type=pl.DeviceIdType.MESH)

    tokens = s_mine.shape[0]
    turn = [lax.rem(y + hop, SIDE) for hop in (*HOPS, 0)]
    loads = [pltpu.make_async_copy(sk_hbm, sketch, load_sem.at[0])]
    for k in range(SIDE):
        span = pl.ds(pl.multiple_of(turn[k] * tokens, tokens), tokens)
        loads.append(pltpu.make_async_copy(o_hbm.at[span, :], o.at[span, :], load_sem.at[1 + k]))
    loads.append(pltpu.make_async_copy(a_hbm, a, load_sem.at[5]))
    for copy in loads:
        copy.start()

    def send_tokens(k):
        span = pl.ds(pl.multiple_of(turn[k] * tokens, tokens), tokens)
        return send(s_part.at[span, :], s_recv.at[k], s_sem, k, along("y", HOPS[k]))

    def share_tokens(sends, factor):
        span = pl.ds(pl.multiple_of(y * tokens, tokens), tokens)
        total = s_part[span, :]
        for k in range(3):
            sends[k].wait_recv()
            total = total + s_recv[k]
        if factor is not None:
            total = lax.dot_general(
                total, factor(), (((1,), (1,)), ((), ())), precision=HIGHEST, preferred_element_type=f32
            )
        s_all[span, :] = total.astype(bf16)
        outs = [send(s_all.at[span, :], s_all.at[span, :], s_sem, 3 + k, along("y", HOPS[k])) for k in range(3)]
        s_t[:, span] = s_all[span, :].T
        for copy, hop in zip(outs, HOPS):
            copy.wait_recv()
            came = pl.ds(pl.multiple_of(lax.rem(y + SIDE - hop, SIDE) * tokens, tokens), tokens)
            s_t[:, came] = s_all[came, :].T
        flush()

    def local_gram(bufs, first, count):
        part = bufs["shard"][first : first + count, :]
        return lax.dot_general(
            part, part, (((0,), (0,)), ((), ())), precision=HIGHEST, preferred_element_type=f32
        )

    def gram_steps():
        h = K // 2
        mine = pl.ds(pl.multiple_of(c * h, h), h)
        theirs = pl.ds(pl.multiple_of((1 - c) * h, h), h)
        copy = send(gram_own.at[theirs, :], gram_first, gram_sem, 0, along("core", 0))
        yield
        copy.wait_recv()
        total = gram_own[mine, :] + gram_first[...]
        thirds = ((0, 24, "xzy"), (24, 24, "zyx"), (48, 16, "yxz"))
        places = {"x": x, "z": z, "y": y}
        totals = [total[first : first + count] for first, count, _ in thirds]
        for stage in range(3):
            copies = []
            for part, (first, count, order) in enumerate(thirds):
                span, place = pl.ds(first, count), places[order[stage]]
                gram_slots[stage, place, span, :] = totals[part]
                for j in HOPS:
                    ref = gram_slots.at[stage, place, span, :]
                    copies.append(send(ref, ref, gram_sem, 2 + 9 * stage + 3 * part + j - 1, along(order[stage], j)))
            yield
            for part, (first, count, order) in enumerate(thirds):
                for copy in copies[3 * part : 3 * part + 3]:
                    copy.wait_recv()
                terms = [gram_slots[stage, i, first : first + count, :] for i in range(SIDE)]
                totals[part] = terms[0] + terms[1] + terms[2] + terms[3]
        total = jnp.concatenate(totals, axis=0)
        gram_half[...] = total
        gram_all[mine, :] = total
        copy = send(gram_half, gram_all.at[mine, :], gram_sem, 1, along("core", 0))
        yield
        copy.wait_recv()
        yield

    def factor_from_gram(row_total, out):
        g = gram_all[...]
        i = lax.broadcasted_iota(jnp.int32, (K, K), 0)
        j = lax.broadcasted_iota(jnp.int32, (K, K), 1)
        on_diagonal = jnp.where(i == j, g, 0.0)
        shift = 1e-5 * jnp.sum(jnp.sum(on_diagonal, axis=1, keepdims=True), axis=0, keepdims=True) / K
        out[...] = inverse_factor(g + jnp.where(i == j, shift, 0.0)) * f32(row_total**0.5)

    def pass_panel(weights, bufs, columns, gather):
        own, c1s, c1r, s2, sem = bufs["own"], bufs["c1s"], bufs["c1r"], bufs["s2"], bufs["sem"]
        a2r, b2r, s3, r3, shard, g = bufs["a2r"], bufs["b2r"], bufs["s3"], bufs["r3"], bufs["shard"], bufs["gathered"]
        rows = own.shape[2]
        large = rows > 256
        waves = wave_rows(rows) if large else (((0, rows // 2), (rows // 2, rows // 2)),)
        zs = [lax.rem(z + 1 + k, SIDE) for k in range(SIDE)]
        span = columns // SIDE
        pieces = 1 if span % 1024 == 0 else 2
        first = []

        def compute(k):
            for piece in range(pieces):
                width = span // pieces
                n = SIDE // pieces
                start = pl.multiple_of(zs[k] * span + piece * width, K)
                r = jnp.dot(s_t[...], weights[:, pl.ds(start, width)], preferred_element_type=f32).T
                r = r.reshape(n, 2, rows, K)
                own[k, piece * n : (piece + 1) * n] = jnp.where(c == 0, r[:, 0], r[:, 1])
                c1s[k, piece * n : (piece + 1) * n] = jnp.where(c == 0, r[:, 1], r[:, 0]).astype(bf16)
            first.append(send(c1s.at[k], c1r.at[k], sem, k, along("core", 0)))

        def add_core(k):
            first[k].wait_recv()
            for i in range(SIDE):
                v = own[k, i] + c1r[k, i].astype(f32)
                own[k, i] = v
                s2[k, i] = v.astype(bf16)

        class Wave:
            def __init__(self, index):
                self.a, self.b = waves[index]
                self.base = 4 + 59 * index
                self.second_a, self.second_b, self.third_a, self.third_b = [], [], [], []
                self.gather_a, self.gather_b, self.on_a, self.on_b, self.cores = [], [], {}, {}, []

            def second(self, k):
                for j in (1, 2, 3):
                    there = lax.rem(x + j, SIDE)
                    self.second_a.append(
                        send(
                            s2.at[k, there, pl.ds(*self.a), :], a2r.at[k, j - 1, pl.ds(*self.a), :],
                            sem, self.base + k * 3 + j - 1, along("x", j),
                        )
                    )
                if k < 3:
                    self.second_b.append(
                        send(
                            s2.at[k, :, pl.ds(*self.b), :], b2r.at[k, :, pl.ds(*self.b), :],
                            sem, self.base + 12 + k, along("z", k + 1),
                        )
                    )

            def third(self):
                part = pl.ds(*self.a)
                for k in range(SIDE):
                    total = own[k, x, part, :]
                    for j in range(3):
                        self.second_a[k * 3 + j].wait_recv()
                        total = total + a2r[k, j, part, :].astype(f32)
                    if k < 3:
                        s3[k, part, :] = total.astype(bf16)
                        self.third_a.append(
                            send(s3.at[k, part, :], r3.at[k, part, :], sem, self.base + 15 + k, along("z", k + 1))
                        )
                    else:
                        shard[part, :] = total
                part = pl.ds(*self.b)
                for k in range(3):
                    self.second_b[k].wait_recv()
                for k in range(SIDE):
                    there = lax.rem(x + 1 + k, SIDE)
                    total = own[3, there, part, :]
                    for j in range(3):
                        total = total + b2r[j, there, part, :].astype(f32)
                    if k < 3:
                        s3[k, part, :] = total.astype(bf16)
                        self.third_b.append(
                            send(s3.at[k, part, :], r3.at[k, part, :], sem, self.base + 18 + k, along("x", k + 1))
                        )
                    else:
                        shard[part, :] = total

            def piece(self, z_, x_, part):
                return g.at[z_, x_, c, pl.ds(*part), :]

            def finish(self):
                for part, copies in ((self.a, self.third_a), (self.b, self.third_b)):
                    part = pl.ds(*part)
                    total = shard[part, :]
                    for k in range(3):
                        copies[k].wait_recv()
                        total = total + r3[k, part, :].astype(f32)
                    shard[part, :] = total
                    if gather:
                        g[z, x, c, part, :] = total.astype(bf16)
                        axis, part, base, outs = (
                            ("z", self.a, 21, self.gather_a) if copies is self.third_a else ("x", self.b, 24, self.gather_b)
                        )
                        for j in (1, 2, 3):
                            ref = self.piece(z, x, part)
                            outs.append(send(ref, ref, sem, self.base + base + j - 1, along(axis, j)))
                if gather:
                    self.forward(0)

            def forward(self, k):
                if k > 0:
                    self.gather_a[k - 1].wait_recv()
                    self.gather_b[k - 1].wait_recv()
                from_z, from_x = lax.rem(z - k + SIDE, SIDE), lax.rem(x - k + SIDE, SIDE)
                for j in (1, 2, 3):
                    ref = self.piece(from_z, x, self.a)
                    self.on_a[k, j] = send(ref, ref, sem, self.base + 27 + k * 3 + j - 1, along("x", j))
                    ref = self.piece(z, from_x, self.b)
                    self.on_b[k, j] = send(ref, ref, sem, self.base + 39 + k * 3 + j - 1, along("z", j))

            def over(self, ref):
                self.cores.append(send(ref, ref, sem, self.base + 51 + len(self.cores), along("core", 0)))

            def first_hop(self):
                for k in (1, 2, 3):
                    self.forward(k)
                self.over(g.at[:, x, c, pl.ds(*self.a), :])
                self.over(g.at[z, :, c, pl.ds(*self.b), :])

            def second_hop(self):
                for j in (1, 2, 3):
                    for k in range(SIDE):
                        self.on_a[k, j].wait_recv()
                    self.over(g.at[:, lax.rem(x - j + SIDE, SIDE), c, pl.ds(*self.a), :])
                    for k in range(SIDE):
                        self.on_b[k, j].wait_recv()
                    self.over(g.at[lax.rem(z - j + SIDE, SIDE), :, c, pl.ds(*self.b), :])

            def wait_cores(self):
                for copy in self.cores:
                    copy.wait_recv()

        parts = [Wave(index) for index in range(len(waves))]
        one, two = parts[0], parts[-1]
        for k in range(SIDE):
            compute(k)
            if k > 0:
                add_core(k - 1)
                one.second(k - 1)
        add_core(3)
        one.second(3)
        if large:
            for k in range(SIDE):
                two.second(k)
            one.third()
        two.third()
        if large:
            one.finish()
            first, count = one.a[0], one.a[1] + one.b[1]
            gram_own[...] = local_gram(bufs, first, count)
            two.finish()
            gram_own[...] += local_gram(bufs, first + count, rows - count)
        else:
            two.finish()
            gram_own[...] = local_gram(bufs, 0, rows)
        steps = gram_steps()
        if not gather:
            return steps
        next(steps)
        next(steps)
        for wave in parts:
            wave.first_hop()
        next(steps)
        for wave in parts:
            wave.second_hop()
        next(steps)
        for wave in parts:
            wave.wait_cores()
        return steps

    row_y, row_z = float(SIDE * features), float(SIDE * hidden)
    for iteration in range(ITERS):
        sends = []
        if iteration == 0:
            loads[0].wait()
            for k in range(SIDE):
                span = pl.ds(pl.multiple_of(turn[k] * tokens, tokens), tokens)
                loads[1 + k].wait()
                s_part[span, :] = jnp.zeros((tokens, K), f32)

                @pl.loop(0, SIDE)
                def _(i):
                    deep = pl.ds(pl.multiple_of(i * (hidden // SIDE), K), hidden // SIDE)
                    s_part[span, :] += jnp.dot(o[span, deep], sketch[deep, :], preferred_element_type=f32)

                if k == 0:
                    pl.semaphore_wait(barrier, len(partners))
                if k < 3:
                    sends.append(send_tokens(k))
            loads[5].wait()
            share_tokens(sends, None)
        else:
            s_part[...] = jnp.zeros(s_part.shape, f32)
            n = hidden // 2

            @pl.loop(0, 2)
            def _(i):
                deep = pl.ds(pl.multiple_of(i * n, K), n)
                block = bufs_z["gathered"][pl.ds(2 * i, 2)].reshape(n, K)
                s_part[...] += jnp.dot(o[:, deep], block, preferred_element_type=f32)

            sends = [send_tokens(k) for k in range(3)]
            for _ in steps:
                pass
            factor_from_gram(row_z, factor_z)
            share_tokens(sends, lambda: factor_z[...])
        steps = pass_panel(a, bufs_y, features, True)
        s_part[...] = jnp.dot(a[...], bufs_y["gathered"][...].reshape(features, K), preferred_element_type=f32)
        sends = [send_tokens(k) for k in range(3)]
        for _ in steps:
            pass
        factor_from_gram(row_y, factor_y)
        share_tokens(sends, lambda: factor_y[...])
        if iteration == ITERS - 1:
            q = lax.dot_general(
                factor_y[...], bufs_y["shard"][...], (((1,), (1,)), ((), ())), precision=HIGHEST, preferred_element_type=f32
            )
            q_ref[...] = q[:RANK, :]
        steps = pass_panel(o, bufs_z, hidden, iteration < ITERS - 1)
    for _ in steps:
        pass
    factor_from_gram(row_z, factor_z)
    p = lax.dot_general(
        factor_z[...], bufs_z["shard"][...], (((1,), (1,)), ((), ())), precision=HIGHEST, preferred_element_type=f32
    )
    p_ref[...] = p[RANK:, :]
    flush()


def copy_out(q_ref, p_ref, q_out, p_out):
    q_out[...] = q_ref[...]
    p_out[...] = p_ref[...]


def panel_scratch(rows):
    return [
        pltpu.VMEM((4, 4, rows, K), f32),
        pltpu.VMEM((4, 4, rows, K), bf16),
        pltpu.VMEM((4, 4, rows, K), bf16),
        pltpu.VMEM((4, 4, rows, K), bf16),
        pltpu.VMEM((4, 3, rows, K), bf16),
        pltpu.VMEM((3, 4, rows, K), bf16),
        pltpu.VMEM((3, rows, K), bf16),
        pltpu.VMEM((3, rows, K), bf16),
        pltpu.VMEM((rows, K), f32),
        pltpu.VMEM((4, 4, 2, rows, K), bf16),
        pltpu.SemaphoreType.DMA((2, 122)),
    ]


def body(activations, out_grads, sketch):
    tokens, features = activations.shape
    hidden = out_grads.shape[1]
    devices = lax.axis_size("dp")
    rows_y, rows_z = features // devices, hidden // devices
    quarter = tokens // SIDE
    scratch = [
        pltpu.VMEM((tokens, features), bf16),
        pltpu.VMEM((tokens, hidden), bf16),
        pltpu.VMEM((hidden, K), bf16),
        pltpu.SemaphoreType.DMA((6,)),
        pltpu.VMEM((tokens, K), f32),
        pltpu.VMEM((3, quarter, K), f32),
        pltpu.VMEM((quarter, K), bf16),
        pltpu.VMEM((tokens, K), bf16),
        pltpu.VMEM((K, tokens), bf16),
        pltpu.SemaphoreType.DMA((2, 6)),
        pltpu.VMEM((K, K), f32),
        pltpu.VMEM((K // 2, K), f32),
        pltpu.VMEM((3, SIDE, K // 2, K), f32),
        pltpu.VMEM((K // 2, K), f32),
        pltpu.VMEM((K, K), f32),
        pltpu.SemaphoreType.DMA((2, 29)),
        pltpu.VMEM((K, K), f32),
        pltpu.VMEM((K, K), f32),
        *panel_scratch(rows_y),
        *panel_scratch(rows_z),
    ]
    q, p = pl.pallas_call(
        functools.partial(kernel, features, hidden),
        out_shape=(
            jax.ShapeDtypeStruct((RANK, rows_y), f32),
            jax.ShapeDtypeStruct((K - RANK, rows_z), f32),
        ),
        in_specs=[pl.BlockSpec(memory_space=pl.ANY)] * 3,
        out_specs=(pl.BlockSpec(memory_space=pltpu.VMEM), pl.BlockSpec(memory_space=pltpu.VMEM)),
        scratch_shapes=scratch,
        compiler_params=pltpu.CompilerParams(
            collective_id=0, has_side_effects=True, vmem_limit_bytes=58 << 20
        ),
        name="subspace_iteration",
    )(activations, out_grads, sketch)
    q, p = pl.pallas_call(
        copy_out,
        out_shape=(jax.ShapeDtypeStruct(q.shape, f32), jax.ShapeDtypeStruct(p.shape, f32)),
        in_specs=[pl.BlockSpec(memory_space=pltpu.VMEM)] * 2,
        out_specs=(pl.BlockSpec(memory_space=pltpu.VMEM), pl.BlockSpec(memory_space=pltpu.VMEM)),
        name="write_outputs",
    )(q, p)
    return q.T, p.T


def solution(mesh):
    return jax.shard_map(
        body,
        mesh=mesh,
        in_specs=(P("dp", "col"), P("dp", "col"), P("col", None)),
        out_specs=(P(("col", "dp"), None), P(("col", "dp"), None)),
        check_vma=False,
    )
```
